128 devices in a mesh: mem: 8 (over x, core), cell: 16 (over y, z).
Axes of the slice: x: 4, y: 4, z: 4, core: 2. Of those that a mesh axis runs over, the one named last changes fastest.
Arguments:
- prior_samples: float32 [512, 256, 512], P('mem', 'cell'), may hold values from -6 to 6
- neighbour_weights: float32 [4, 256, 512], P(None, 'cell'), may hold values from 0.02 to 0.22
- obs_cell: int32 [4, 128], replicated, may hold values from 0 to 131071
- obs_value: float32 [4, 128], replicated, may hold values from -8 to 8
- obs_var: float32 [4, 128], replicated, may hold values from 0.1 to 1
- block_order: int32 [4], replicated, may hold values from 0 to 3, each once
Outputs:
- analysis: float32 [512, 256, 512], P('mem', 'cell')
The draws below stay inside these ranges and needn't reach their ends.
Inputs may be any that keep to these rules, and one draw needn't show every extreme that they name: `block_order`: each block number appears once.
All inputs are finite; a program needn't handle non-finite values.
Results may differ from the reference program's by a relative error of at most 0.00014.
Values sent between devices are 32-bit elements; how exact they have to be, the bound alone decides.
No kernel may reach another device: no remote copies, remote signals or barrier semaphores. Data moves between devices by JAX's collectives and lax.ppermute only.
A program may use at most 128 MiB of HBM per device.

```python
import math
import jax
import jax.numpy as jnp
from jax import lax

SAMPLE_TOTAL = 512
NOBS = 128
NBLK = 4
SLAB_WIDTH_SITES = 512
SLAB_HEIGHT = 256


def with_ends(array, own_key, low, top_value):
    dims = array.shape
    index_at = [jax.random.randint(jax.random.fold_in(own_key, axis), (), 0, dims[axis]) for axis in range(len(dims))]
    array = array.at[tuple(index_at)].set(low)
    longest = dims.index(max(dims))
    index_at[longest] = (index_at[longest] + 1) % dims[longest]
    return array.at[tuple(index_at)].set(top_value)


def block_scale(stream_key, shape, pieces, least, largest):
    gain = 1.0
    for axis_at, parts in pieces:
        heights = jax.random.uniform(jax.random.fold_in(jax.random.fold_in(stream_key, 6), axis_at), (parts,), jnp.float32, least / len(pieces), largest / len(pieces))
        gain = gain * jnp.repeat(jnp.exp(heights), shape[axis_at] // parts).reshape((-1,) + (1,) * (len(shape) - 1 - axis_at))
    return gain


def noise(stream_key, shape, width, reach, shards=(), kind=jnp.bfloat16):
    values = jax.random.normal(stream_key, shape, jnp.float32) * width
    if len(shards) > 0:
        values = block_scale(stream_key, shape, shards, -0.22, 0.18) * values
    return jnp.clip(values, min=-reach, max=reach).astype(kind)


def setup_inputs(seed: int = 0) -> dict:
    splits = jax.random.split(jax.random.key(seed), 7)
    prior_samples = noise(splits[0], (SAMPLE_TOTAL, SLAB_HEIGHT, SLAB_WIDTH_SITES), 1.0, 6.0, ((0, 8), (1, 16)), jnp.float32)
    neighbour_weights = jnp.clip(jnp.exp(math.log(0.22) - 2.3978953 * jax.random.uniform(splits[1], (4, SLAB_HEIGHT, SLAB_WIDTH_SITES), jnp.float32) ** block_scale(splits[1], (4, SLAB_HEIGHT, SLAB_WIDTH_SITES), ((1, 16),), -0.2, 0.2)), 0.02, 0.22)
    obs_cell = with_ends(jax.random.randint(splits[2], (NBLK, NOBS), 0, SLAB_HEIGHT * SLAB_WIDTH_SITES), jax.random.fold_in(splits[2], 1), 0, (SLAB_HEIGHT * SLAB_WIDTH_SITES) - 1).astype(jnp.int32)
    obs_value = noise(splits[3], (NBLK, NOBS), 1.5, 8.0, (), jnp.float32)
    obs_var = jnp.clip(jnp.exp(jax.random.uniform(splits[4], (NBLK, NOBS), jnp.float32, math.log(0.1), math.log(1.0))), 0.1, 1.0)
    block_order = jax.random.permutation(splits[5], NBLK).astype(jnp.int32)
    return {"prior_samples": prior_samples, "neighbour_weights": neighbour_weights, "obs_cell": obs_cell, "obs_value": obs_value, "obs_var": obs_var, "block_order": block_order}


def predicted_field(prior_samples, neighbour_weights):
    padded = jnp.pad(prior_samples, ((0, 0), (1, 1), (1, 1)))
    to_east = padded[:, 1:-1, 2:]
    to_west = padded[:, 1:-1, :-2]
    to_north = padded[:, :-2, 1:-1]
    to_south = padded[:, 2:, 1:-1]
    return prior_samples + neighbour_weights[0] * (to_east - prior_samples) + neighbour_weights[1] * (to_west - prior_samples) + neighbour_weights[2] * (to_north - prior_samples) + neighbour_weights[3] * (to_south - prior_samples)

def tri_solve(update_matrix, right, transposed):
    return lax.linalg.triangular_solve(update_matrix, right, left_side=True, lower=True, transpose_a=transposed)

def reference(prior_samples, neighbour_weights, obs_cell, obs_value, obs_var, block_order):
    highest = lax.Precision.HIGHEST
    raveled_field = predicted_field(prior_samples, neighbour_weights).reshape(SAMPLE_TOTAL, SLAB_HEIGHT * SLAB_WIDTH_SITES)
    ens_mean = lax.optimization_barrier(jnp.sum(raveled_field, axis=0)) / SAMPLE_TOTAL
    anomaly = raveled_field - ens_mean

    def one_block(carry, block):
        ens_mean, anomaly = carry
        observed = obs_cell[block]
        noise_var = obs_var[block]
        prior_rows = anomaly[:, observed]
        prior_mean = ens_mean[observed]
        innov = obs_value[block] - prior_mean
        spread = jnp.dot(prior_rows.T, prior_rows, precision=highest) / (SAMPLE_TOTAL - 1) + jnp.diag(noise_var)
        factor_low = jnp.linalg.cholesky(spread)
        factor_sum = factor_low + jnp.diag(jnp.sqrt(noise_var))
        halfway = tri_solve(factor_low, innov[:, None], False)
        weights = tri_solve(factor_low, halfway, True)[:, 0]
        cross = jnp.dot(prior_rows.T, anomaly, precision=highest)
        ens_mean = ens_mean + jnp.dot(weights, cross, precision=highest) / (SAMPLE_TOTAL - 1)
        scaled = tri_solve(factor_low, cross, False) / (SAMPLE_TOTAL - 1)
        mapped = tri_solve(factor_sum, prior_rows.T, False)
        anomaly = anomaly - jnp.dot(mapped.T, scaled, precision=highest)
        return ((ens_mean, anomaly), None)
    (ens_mean, anomaly), unused = lax.scan(one_block, (ens_mean, anomaly), block_order)
    return (ens_mean + anomaly).reshape(SAMPLE_TOTAL, SLAB_HEIGHT, SLAB_WIDTH_SITES)
```

```python
import functools

import jax
import jax.numpy as jnp
from jax import lax
from jax.experimental import pallas as pl
from jax.experimental.pallas import tpu as pltpu
from jax.sharding import PartitionSpec as P

SAMPLE_TOTAL = 512
NOBS = 128
ALL_OBS = 512
HIGHEST = lax.Precision.HIGHEST
NT = (((1,), (1,)), ((), ()))
TN = (((0,), (0,)), ((), ()))
NN = (((1,), (0,)), ((), ()))
VMEM_LIMIT = 48 * 1024 * 1024


def halves(value):
    high = value.astype(jnp.bfloat16)
    low = (value - high.astype(jnp.float32)).astype(jnp.bfloat16)
    return high, low


def dot_split(left, right, dims):
    f32 = jnp.float32
    left_high, left_low = left
    right_high, right_low = right
    small = lax.dot_general(left_low, right_high, dims, preferred_element_type=f32)
    small = small + lax.dot_general(left_high, right_low, dims, preferred_element_type=f32)
    return small + lax.dot_general(left_high, right_high, dims, preferred_element_type=f32)


def dot3(left, right, dims):
    return dot_split(halves(left), halves(right), dims)


def dot6(left, right, dims):
    return lax.dot_general(
        left, right, dims, precision=HIGHEST, preferred_element_type=jnp.float32
    )


def forecast_kernel(x_ref, low_ref, high_ref, weight_ref, row_ref, col_ref, pieces_ref, seen_ref, flat_ref):
    members, rows, width = x_ref.shape
    row_at = lax.broadcasted_iota(jnp.int32, (rows, width), 0)
    col_at = lax.broadcasted_iota(jnp.int32, (rows, width), 1)
    east, west, north, south = [weight_ref[i] for i in range(4)]

    def member(m, carry):
        x = x_ref[m]
        to_east = jnp.where(col_at == width - 1, 0.0, pltpu.roll(x, width - 1, 1))
        to_west = jnp.where(col_at == 0, 0.0, pltpu.roll(x, 1, 1))
        to_north = jnp.where(row_at == 0, low_ref[m], pltpu.roll(x, 1, 0))
        to_south = jnp.where(row_at == rows - 1, high_ref[m], pltpu.roll(x, rows - 1, 0))
        f = (
            x
            + east * (to_east - x)
            + west * (to_west - x)
            + north * (to_north - x)
            + south * (to_south - x)
        )
        flat_ref[pl.ds(pl.multiple_of(m * rows, rows), rows), :] = f
        for h in range(2):
            for q in range(4):
                pieces_ref[4 * h + q, m] = f[8 * h : 8 * h + 8, 128 * q : 128 * q + 128]
        return carry

    lax.fori_loop(0, members, member, 0, unroll=4)
    pick = (lax.broadcasted_iota(jnp.int32, (width, ALL_OBS), 0) == col_ref[...]).astype(jnp.bfloat16)
    own_row = (lax.broadcasted_iota(jnp.int32, (rows, ALL_OBS), 0) == row_ref[...]).astype(jnp.float32)
    part = 8

    def select(g, carry):
        value = flat_ref[pl.ds(pl.multiple_of(g * part * rows, part * rows), part * rows), :]
        total = None
        for _ in range(3):
            cut = value.astype(jnp.bfloat16)
            value = value - cut.astype(jnp.float32)
            term = lax.dot_general(cut, pick, NN, preferred_element_type=jnp.float32)
            total = term if total is None else total + term
        total = total.reshape(part, rows, ALL_OBS) * own_row[None]
        seen_ref[pl.ds(pl.multiple_of(g * part, part), part), :] = jnp.sum(total, axis=1)
        return carry

    lax.fori_loop(0, members // part, select, 0, unroll=2)


def over_rows(value, row):
    return jnp.broadcast_to(value[row : row + 1, :], (8, NOBS))


def over_lanes(value, lane):
    return jnp.broadcast_to(value[:, lane : lane + 1], (8, NOBS))


def factor(block, root):
    count = NOBS // 8
    sub = lax.broadcasted_iota(jnp.int32, (8, NOBS), 0)
    lane = lax.broadcasted_iota(jnp.int32, (8, NOBS), 1)
    rows = [block[8 * i : 8 * i + 8, :] for i in range(count)]
    shifted = [(lane == sub + 8 * i).astype(jnp.float32) for i in range(count)]
    inverse = [None] * count
    for b in range(count):
        panel = rows[b]
        column = [over_lanes(panel, 8 * b + k) for k in range(8)]
        done = jnp.zeros((8, NOBS), jnp.float32)
        plus = shifted[b]
        inv_roots = []
        for k in range(8):
            at = 8 * b + k
            pivot = over_rows(column[k], k)
            inv = 1.0 / pivot
            inv_root = lax.rsqrt(pivot)
            inv_roots.append(inv_root)
            row = jnp.where(lane == at, 1.0, over_rows(panel, k))
            done = jnp.where(sub == k, row * inv_root, done)
            scaled = row * inv
            away = jnp.where(sub == k, -1.0, column[k])
            panel = jnp.where((sub == k) | (lane == at), 0.0, panel) - away * scaled
            plus_row = over_rows(plus, k) / (pivot * inv_root + over_rows(root[8 * b : 8 * b + 8, :], k))
            below = jnp.where(sub > k, column[k] * inv_root, 0.0)
            plus = jnp.where(sub == k, plus_row, plus - below * plus_row)
            for j in range(k + 1, 8):
                step = over_rows(column[j], k) * inv
                column[j] = jnp.where(sub == k, 0.0, column[j]) - away * step
        inverse[b] = jnp.where(lane <= sub + 8 * b, done, 0.0)
        shifted[b] = plus
        if b == count - 1:
            break
        for k in reversed(range(8)):
            above = jnp.where(sub < k, over_lanes(done, 8 * b + k), 0.0)
            row = over_rows(plus, k) * inv_roots[k]
            plus = jnp.where(sub == k, row, plus - above * row)
        panel_rows = [over_rows(panel, k) for k in range(8)]
        plus_rows = [over_rows(plus, k) for k in range(8)]
        inside = (lane >= 8 * b) & (lane < 8 * b + 8)
        for r in range(b + 1, count):
            left = [over_lanes(rows[r], 8 * b + k) for k in range(8)]
            new = jnp.where(inside, 0.0, rows[r])
            new_shifted = shifted[r]
            for k in range(8):
                new = new - left[k] * panel_rows[k]
                new_shifted = new_shifted - left[k] * plus_rows[k]
            rows[r] = new
            shifted[r] = new_shifted
    return jnp.concatenate(inverse, axis=0), jnp.concatenate(shifted, axis=0)


def transform_kernel(seen_ref, value_ref, var_ref, root_ref, high_ref, low_ref, cov_ref, state_ref, gain_ref, minus_ref):
    n = ALL_OBS
    blocks = n // NOBS
    seen = seen_ref[...]
    mean = jnp.sum(seen, axis=0, keepdims=True) / SAMPLE_TOTAL
    anomaly = seen - mean
    state_ref[0:SAMPLE_TOTAL, :] = anomaly
    state_ref[SAMPLE_TOTAL:, :] = jnp.broadcast_to(value_ref[...] - mean, (8, n))
    minus_ref[...] = anomaly
    cov = dot6(anomaly, anomaly, TN) / (SAMPLE_TOTAL - 1)
    eye = lax.broadcasted_iota(jnp.int32, (n, n), 0) == lax.broadcasted_iota(jnp.int32, (n, n), 1)
    cov_ref[...] = cov + jnp.where(eye, var_ref[...], 0.0)
    for j in range(blocks):
        low, high = NOBS * j, NOBS * (j + 1)
        inv_low, inv_sum = factor(cov_ref[low:high, low:high], root_ref[low:high, :])
        rest = high < n
        if rest:
            below = dot6(cov_ref[high:, low:high], inv_low, NT)
            cov_ref[high:, high:] = cov_ref[high:, high:] - dot6(below, below, NT)
            below = halves(below)
        inv_low, inv_sum = halves(inv_low), halves(inv_sum)
        gain = dot_split(halves(state_ref[:, low:high]), inv_low, NT)
        minus = dot_split(halves(minus_ref[:, low:high]), inv_sum, NT)
        gain_ref[:, low:high] = gain
        if rest:
            state_ref[:, high:] = state_ref[:, high:] - dot_split(halves(gain), below, NT)
            minus_ref[:, high:] = minus_ref[:, high:] - dot_split(halves(minus), below, NT)
        minus_ref[:, low:high] = minus
    mean_step = gain_ref[SAMPLE_TOTAL : SAMPLE_TOTAL + 1, :]
    left = (mean_step - minus_ref[...]) * (1.0 / (SAMPLE_TOTAL - 1))
    total = dot3(left, gain_ref[0:SAMPLE_TOTAL, :], NT)
    high_part, low_part = halves(total)
    high_ref[...] = high_part
    low_ref[...] = low_part


def update_kernel(high_ref, low_ref, cells_ref, out_ref):
    transform = (high_ref[...], low_ref[...])
    for r in range(0, 8, 2):
        field = jnp.concatenate(
            [cells_ref[pl.ds(r + i, SAMPLE_TOTAL, stride=8), :] for i in range(2)], axis=1
        )
        new = field + dot_split(transform, halves(field), NN)
        for i in range(2):
            out_ref[pl.ds(r + i, SAMPLE_TOTAL, stride=8), :] = new[:, 128 * i : 128 * i + 128]


def call(kernel, out_shape, scratch=(), flops=0, bytes_accessed=0):
    return pl.pallas_call(
        kernel,
        out_shape=out_shape,
        scratch_shapes=list(scratch),
        compiler_params=pltpu.CompilerParams(vmem_limit_bytes=VMEM_LIMIT),
        cost_estimate=pl.CostEstimate(flops=flops, bytes_accessed=bytes_accessed, transcendentals=0),
    )


def body(prior_samples, neighbour_weights, obs_cell, obs_value, obs_var, block_order):
    f32 = jnp.float32
    members_dev, tile_rows, width = prior_samples.shape
    mem_count, cell_count = lax.axis_size("mem"), lax.axis_size("cell")
    forward = [(i, i + 1) for i in range(cell_count - 1)]
    backward = [(i + 1, i) for i in range(cell_count - 1)]
    low = lax.ppermute(prior_samples[:, -1:, :], "cell", forward)
    high = lax.ppermute(prior_samples[:, :1, :], "cell", backward)
    cell = obs_cell[block_order].reshape(1, ALL_OBS)
    value = obs_value[block_order].reshape(1, ALL_OBS)
    var = obs_var[block_order].reshape(1, ALL_OBS)
    root = jnp.broadcast_to(jnp.sqrt(var).reshape(ALL_OBS, 1), (ALL_OBS, NOBS))
    row = cell // width - lax.axis_index("cell") * tile_rows
    col = cell % width

    pieces, seen = call(
        forecast_kernel,
        (
            jax.ShapeDtypeStruct((mem_count, members_dev, 8, 128), f32),
            jax.ShapeDtypeStruct((members_dev, ALL_OBS), f32),
        ),
        [pltpu.VMEM((members_dev * tile_rows, width), f32)],
    )(prior_samples, low, high, neighbour_weights, row, col)

    share = members_dev // cell_count
    seen = lax.all_to_all(seen.reshape(cell_count, share, ALL_OBS), "cell", 0, 0)
    seen = jnp.sum(seen, axis=0)
    seen = lax.all_to_all(jnp.broadcast_to(seen[None], (cell_count,) + seen.shape), "cell", 0, 0)
    seen = seen.reshape(members_dev, ALL_OBS)
    seen = lax.all_to_all(jnp.broadcast_to(seen[None], (mem_count,) + seen.shape), "mem", 0, 0)
    seen = seen.reshape(SAMPLE_TOTAL, ALL_OBS)
    cells = lax.all_to_all(pieces, "mem", 0, 0)

    square = (ALL_OBS, ALL_OBS)
    transform = call(
        transform_kernel,
        (jax.ShapeDtypeStruct(square, jnp.bfloat16),) * 2,
        [
            pltpu.VMEM(square, f32),
            pltpu.VMEM((SAMPLE_TOTAL + 8, ALL_OBS), f32),
            pltpu.VMEM((SAMPLE_TOTAL + 8, ALL_OBS), f32),
            pltpu.VMEM(square, f32),
        ],
        flops=20_000_000_000,
        bytes_accessed=2_000_000,
    )(seen, value, var, root)

    cells = cells.reshape(SAMPLE_TOTAL * 8, 128)
    new = call(update_kernel, jax.ShapeDtypeStruct(cells.shape, f32))(*transform, cells)
    new = lax.all_to_all(new.reshape(mem_count, members_dev, 8, 128), "mem", 0, 0)
    new = new.reshape(2, 4, members_dev, 8, 128).transpose(2, 0, 3, 1, 4)
    return new.reshape(prior_samples.shape)


def solution(mesh):
    return jax.shard_map(
        body,
        mesh=mesh,
        in_specs=(P("mem", "cell", None), P(None, "cell", None), P(), P(), P(), P()),
        out_specs=P("mem", "cell", None),
        check_vma=False,
    )
```

```python
import functools

import jax
import jax.numpy as jnp
from jax import lax
from jax.experimental import pallas as pl
from jax.experimental.pallas import tpu as pltpu
from jax.sharding import PartitionSpec as P

SAMPLE_TOTAL = 512
NOBS = 128
ALL_OBS = 512
HIGHEST = lax.Precision.HIGHEST
NT = (((1,), (1,)), ((), ()))
TN = (((0,), (0,)), ((), ()))
NN = (((1,), (0,)), ((), ()))
VMEM_LIMIT = 48 * 1024 * 1024
INNER = tuple(range(4, 12))
OUTER = (0, 1, 2, 3, 12, 13, 14, 15)


def halves(value):
    high = value.astype(jnp.bfloat16)
    low = (value - high.astype(jnp.float32)).astype(jnp.bfloat16)
    return high, low


def dot_split(left, right, dims):
    f32 = jnp.float32
    left_high, left_low = left
    right_high, right_low = right
    small = lax.dot_general(left_low, right_high, dims, preferred_element_type=f32)
    small = small + lax.dot_general(left_high, right_low, dims, preferred_element_type=f32)
    return small + lax.dot_general(left_high, right_high, dims, preferred_element_type=f32)


def dot3(left, right, dims):
    return dot_split(halves(left), halves(right), dims)


def dot6(left, right, dims):
    return lax.dot_general(
        left, right, dims, precision=HIGHEST, preferred_element_type=jnp.float32
    )


def forecast_kernel(x_ref, weight_ref, row_ref, col_ref, inner_ref, outer_ref, edge_ref, seen_ref, flat_ref, own_ref, raw_ref):
    members, rows, width = x_ref.shape
    col_at = lax.broadcasted_iota(jnp.int32, (rows, width), 1)
    row_at = lax.broadcasted_iota(jnp.int32, (rows, width), 0)
    east, west, north, south = [weight_ref[i] for i in range(4)]

    def member(m, carry):
        x = x_ref[m]
        to_east = jnp.where(col_at == width - 1, 0.0, pltpu.roll(x, width - 1, 1))
        to_west = jnp.where(col_at == 0, 0.0, pltpu.roll(x, 1, 1))
        to_north = jnp.where(row_at == 0, 0.0, pltpu.roll(x, 1, 0))
        to_south = jnp.where(row_at == rows - 1, 0.0, pltpu.roll(x, rows - 1, 0))
        f = (
            x
            + east * (to_east - x)
            + west * (to_west - x)
            + north * (to_north - x)
            + south * (to_south - x)
        )
        for q in range(4):
            at = pl.multiple_of(q * members * rows + m * rows, rows)
            flat_ref[pl.ds(at, rows), :] = f[:, 128 * q : 128 * q + 128]
        return carry

    lax.fori_loop(0, members, member, 0, unroll=4)
    pick = (lax.broadcasted_iota(jnp.int32, (width, ALL_OBS), 0) == col_ref[...]).astype(jnp.bfloat16)
    at_row = row_ref[...]
    own_row = (lax.broadcasted_iota(jnp.int32, (rows, ALL_OBS), 0) == at_row).astype(jnp.float32)
    part = 8

    def picked(value):
        total = None
        for _ in range(3):
            cut = value.astype(jnp.bfloat16)
            value = value - cut.astype(jnp.float32)
            term = lax.dot_general(cut, pick, NN, preferred_element_type=jnp.float32)
            total = term if total is None else total + term
        return total

    def select(g, carry):
        start = [q * members * rows + g * part * rows for q in range(4)]
        value = [flat_ref[pl.ds(pl.multiple_of(at, part * rows), part * rows), :] for at in start]
        value = jnp.concatenate(value, axis=1)
        total = picked(value).reshape(part, rows, ALL_OBS) * own_row[None]
        own_ref[pl.ds(pl.multiple_of(g * part, part), part), :] = jnp.sum(total, axis=1)
        return carry

    lax.fori_loop(0, members // part, select, 0, unroll=2)
    top, bottom = x_ref[:, 0, :], x_ref[:, rows - 1, :]
    edge_ref[0] = top
    edge_ref[1] = bottom
    raw_ref[...] = jnp.where(at_row == -1, picked(top), 0.0) + jnp.where(at_row == rows, picked(bottom), 0.0)
    weight = jnp.concatenate([north[0:8], south[rows - 8 :]], axis=0)
    weight = picked(weight)
    weight = jnp.where(at_row == 0, weight[0:1], 0.0) + jnp.where(at_row == rows - 1, weight[15:16], 0.0)
    groups, share = seen_ref.shape[0], members // seen_ref.shape[0]
    for q in range(4):
        lanes = slice(128 * q, 128 * q + 128)
        for g in range(groups):
            seen_ref[g, share * q : share * q + share, :] = own_ref[share * g : share * g + share, lanes]
            seen_ref[g, 16 + share * q : 16 + share * q + share, :] = raw_ref[share * g : share * g + share, lanes]
            seen_ref[g, 32 + q : 33 + q, :] = weight[:, lanes]
    for g in range(groups):
        seen_ref[g, 36:40, :] = jnp.zeros((4, 128), jnp.float32)
    for r in range(rows):
        for q in range(4):
            value = flat_ref[pl.ds(q * members * rows + r, members, stride=rows), :]
            lanes = slice(128 * q, 128 * q + 128)
            if r in INNER:
                at = width * (r - INNER[0])
                inner_ref[:, at + 128 * q : at + 128 * q + 128] = value
            else:
                outer_ref[OUTER.index(r), :, lanes] = value


def seen_kernel(parts_ref, out_ref):
    total = parts_ref[0]
    for i in range(1, parts_ref.shape[0]):
        total = total + parts_ref[i]
    for q in range(4):
        own = total[4 * q : 4 * q + 4]
        raw = total[16 + 4 * q : 20 + 4 * q]
        out_ref[:, 128 * q : 128 * q + 128] = own + raw * total[32 + q : 33 + q]


def over_rows(value, row):
    return jnp.broadcast_to(value[row : row + 1, :], (8, NOBS))


def over_lanes(value, lane):
    return jnp.broadcast_to(value[:, lane : lane + 1], (8, NOBS))


def factor(block, root):
    count = NOBS // 8
    sub = lax.broadcasted_iota(jnp.int32, (8, NOBS), 0)
    lane = lax.broadcasted_iota(jnp.int32, (8, NOBS), 1)
    rows = [block[8 * i : 8 * i + 8, :] for i in range(count)]
    shifted = [(lane == sub + 8 * i).astype(jnp.float32) for i in range(count)]
    inverse = [None] * count
    for b in range(count):
        panel = rows[b]
        column = [over_lanes(panel, 8 * b + k) for k in range(8)]
        done = jnp.zeros((8, NOBS), jnp.float32)
        plus = shifted[b]
        inv_roots = []
        for k in range(8):
            at = 8 * b + k
            pivot = over_rows(column[k], k)
            inv = 1.0 / pivot
            inv_root = lax.rsqrt(pivot)
            inv_roots.append(inv_root)
            row = jnp.where(lane == at, 1.0, over_rows(panel, k))
            done = jnp.where(sub == k, row * inv_root, done)
            scaled = row * inv
            away = jnp.where(sub == k, -1.0, column[k])
            panel = jnp.where((sub == k) | (lane == at), 0.0, panel) - away * scaled
            plus_row = over_rows(plus, k) / (pivot * inv_root + over_rows(root[8 * b : 8 * b + 8, :], k))
            below = jnp.where(sub > k, column[k] * inv_root, 0.0)
            plus = jnp.where(sub == k, plus_row, plus - below * plus_row)
            for j in range(k + 1, 8):
                step = over_rows(column[j], k) * inv
                column[j] = jnp.where(sub == k, 0.0, column[j]) - away * step
        inverse[b] = jnp.where(lane <= sub + 8 * b, done, 0.0)
        shifted[b] = plus
        if b == count - 1:
            break
        for k in reversed(range(8)):
            above = jnp.where(sub < k, over_lanes(done, 8 * b + k), 0.0)
            row = over_rows(plus, k) * inv_roots[k]
            plus = jnp.where(sub == k, row, plus - above * row)
        panel_rows = [over_rows(panel, k) for k in range(8)]
        plus_rows = [over_rows(plus, k) for k in range(8)]
        inside = (lane >= 8 * b) & (lane < 8 * b + 8)
        for r in range(b + 1, count):
            left = [over_lanes(rows[r], 8 * b + k) for k in range(8)]
            new = jnp.where(inside, 0.0, rows[r])
            new_shifted = shifted[r]
            for k in range(8):
                new = new - left[k] * panel_rows[k]
                new_shifted = new_shifted - left[k] * plus_rows[k]
            rows[r] = new
            shifted[r] = new_shifted
    return jnp.concatenate(inverse, axis=0), jnp.concatenate(shifted, axis=0)


def transform_kernel(order_ref, seen_ref, value_ref, var_ref, root_ref, high_ref, low_ref, cov_ref, state_ref, gain_ref, minus_ref):
    n = ALL_OBS
    blocks = n // NOBS
    slots, share = seen_ref.shape[0], seen_ref.shape[1]
    total = seen_ref[0]
    for s in range(1, slots):
        total = total + seen_ref[s]
    mean = jnp.sum(total, axis=0, keepdims=True) / SAMPLE_TOTAL
    for s in range(slots):
        state_ref[pl.ds(pl.multiple_of(order_ref[s] * share, share), share), :] = seen_ref[s] - mean
    state_ref[SAMPLE_TOTAL:, :] = jnp.broadcast_to(value_ref[...] - mean, (8, n))
    anomaly = state_ref[0:SAMPLE_TOTAL, :]
    minus_ref[...] = anomaly
    cov = dot6(anomaly, anomaly, TN) / (SAMPLE_TOTAL - 1)
    eye = lax.broadcasted_iota(jnp.int32, (n, n), 0) == lax.broadcasted_iota(jnp.int32, (n, n), 1)
    cov_ref[...] = cov + jnp.where(eye, var_ref[...], 0.0)
    for j in range(blocks):
        low, high = NOBS * j, NOBS * (j + 1)
        inv_low, inv_sum = factor(cov_ref[low:high, low:high], root_ref[low:high, :])
        rest = high < n
        if rest:
            below = dot6(cov_ref[high:, low:high], inv_low, NT)
            cov_ref[high:, high:] = cov_ref[high:, high:] - dot6(below, below, NT)
            below = halves(below)
        inv_low, inv_sum = halves(inv_low), halves(inv_sum)
        gain = dot_split(halves(state_ref[:, low:high]), inv_low, NT)
        minus = dot_split(halves(minus_ref[:, low:high]), inv_sum, NT)
        gain_ref[:, low:high] = gain
        if rest:
            state_ref[:, high:] = state_ref[:, high:] - dot_split(halves(gain), below, NT)
            minus_ref[:, high:] = minus_ref[:, high:] - dot_split(halves(minus), below, NT)
        minus_ref[:, low:high] = minus
    mean_step = gain_ref[SAMPLE_TOTAL : SAMPLE_TOTAL + 1, :]
    left = (mean_step - minus_ref[...]) * (1.0 / (SAMPLE_TOTAL - 1))
    total = dot3(left, gain_ref[0:SAMPLE_TOTAL, :], NT)
    high_part, low_part = halves(total)
    high_ref[...] = high_part
    low_ref[...] = low_part


def outer_kernel(high_ref, low_ref, cells_ref, out_ref):
    field = cells_ref[...]
    out_ref[...] = field + dot_split((high_ref[...], low_ref[...]), halves(field), NN)


def inner_kernel(place_ref, high_ref, low_ref, own_ref, cells_ref, out_ref):
    out_ref[...] = own_ref[...] + dot_split(
        (high_ref[...], low_ref[...]), halves(cells_ref[...]), NN
    )


def join_kernel(inner_ref, outer_ref, out_ref, flat_ref):
    members = inner_ref.shape[0]
    width = outer_ref.shape[2]
    count = out_ref.shape[0]
    rows = count // members
    for r in range(rows):
        if r in INNER:
            value = inner_ref[:, width * (r - INNER[0]) : width * (r - INNER[0] + 1)]
        else:
            value = outer_ref[OUTER.index(r)]
        for q in range(width // 128):
            at = pl.ds(q * count + r, members, stride=rows)
            flat_ref[at, :] = value[:, 128 * q : 128 * q + 128]
    for q in range(width // 128):
        out_ref[:, 128 * q : 128 * q + 128] = flat_ref[count * q : count * (q + 1), :]


def call(kernel, out_shape, scratch=(), flops=0, bytes_accessed=0, in_specs=None):
    extra = {} if in_specs is None else {"in_specs": in_specs}
    return pl.pallas_call(
        kernel,
        out_shape=out_shape,
        scratch_shapes=list(scratch),
        compiler_params=pltpu.CompilerParams(vmem_limit_bytes=VMEM_LIMIT),
        cost_estimate=pl.CostEstimate(flops=flops, bytes_accessed=bytes_accessed, transcendentals=0),
        **extra,
    )


def body(prior_samples, neighbour_weights, obs_cell, obs_value, obs_var, block_order):
    f32 = jnp.float32
    members_dev, tile_rows, width = prior_samples.shape
    mem_count, cell_count = lax.axis_size("mem"), lax.axis_size("cell")
    me = lax.axis_index("mem")
    cell = obs_cell[block_order].reshape(1, ALL_OBS)
    value = obs_value[block_order].reshape(1, ALL_OBS)
    var = obs_var[block_order].reshape(1, ALL_OBS)
    root = jnp.broadcast_to(jnp.sqrt(var).reshape(ALL_OBS, 1), (ALL_OBS, NOBS))
    row = cell // width - lax.axis_index("cell") * tile_rows
    col = cell % width
    share = members_dev // cell_count
    inner_cells = len(INNER) * width

    inner, outer, edge, seen = call(
        forecast_kernel,
        (
            jax.ShapeDtypeStruct((members_dev, inner_cells), f32),
            jax.ShapeDtypeStruct((len(OUTER), members_dev, width), f32),
            jax.ShapeDtypeStruct((2, members_dev, width), f32),
            jax.ShapeDtypeStruct((cell_count, 40, 128), f32),
        ),
        [
            pltpu.VMEM((members_dev * tile_rows * 4, 128), f32),
            pltpu.VMEM((members_dev, ALL_OBS), f32),
            pltpu.VMEM((members_dev, ALL_OBS), f32),
        ],
    )(prior_samples, neighbour_weights, row, col)

    seen = lax.all_to_all(seen, "cell", 0, 0)
    all_inner = lax.all_gather(inner, "mem", tiled=True)
    forward = [(i, i + 1) for i in range(cell_count - 1)]
    backward = [(i + 1, i) for i in range(cell_count - 1)]
    low = lax.ppermute(edge[1], "cell", forward)
    high = lax.ppermute(edge[0], "cell", backward)
    last = len(OUTER) - 1
    outer = outer.at[0].add(neighbour_weights[2, 0] * low)
    outer = outer.at[last].add(neighbour_weights[3, tile_rows - 1] * high)
    cells = lax.all_to_all(outer, "mem", 0, 0)

    seen = call(seen_kernel, jax.ShapeDtypeStruct((share, ALL_OBS), f32))(seen)
    seen = lax.all_to_all(jnp.broadcast_to(seen[None], (cell_count,) + seen.shape), "cell", 0, 0)
    seen = seen.reshape(1, members_dev, ALL_OBS)
    turns = [
        lax.ppermute(seen, "mem", [(i, (i + 2 * d) % mem_count) for i in range(mem_count)])
        for d in range(1, mem_count // 2)
    ]
    seen = jnp.concatenate([seen] + turns, axis=0)
    other = lax.ppermute(seen, "mem", [(i, i ^ 1) for i in range(mem_count)])
    seen = jnp.concatenate([seen, other], axis=0)
    turn = jnp.arange(mem_count // 2, dtype=jnp.int32)
    order = (me - 2 * turn) % mem_count
    order = jnp.concatenate([order, order ^ 1])

    square = (ALL_OBS, ALL_OBS)
    vmem = pl.BlockSpec(memory_space=pltpu.VMEM)
    high_part, low_part = call(
        transform_kernel,
        (jax.ShapeDtypeStruct(square, jnp.bfloat16),) * 2,
        [
            pltpu.VMEM(square, f32),
            pltpu.VMEM((SAMPLE_TOTAL + 8, ALL_OBS), f32),
            pltpu.VMEM((SAMPLE_TOTAL + 8, ALL_OBS), f32),
            pltpu.VMEM(square, f32),
        ],
        flops=20_000_000_000,
        bytes_accessed=2_000_000,
        in_specs=[pl.BlockSpec(memory_space=pltpu.SMEM)] + [vmem] * 4,
    )(order, seen, value, var, root)

    new = call(outer_kernel, jax.ShapeDtypeStruct((SAMPLE_TOTAL, width), f32))(
        high_part, low_part, cells.reshape(SAMPLE_TOTAL, width)
    )
    new = lax.all_to_all(new.reshape(mem_count, members_dev, width), "mem", 0, 0)

    block = 1024
    mine = pl.BlockSpec((members_dev, ALL_OBS), lambda i, place: (place[0], 0))
    inner = pl.pallas_call(
        inner_kernel,
        out_shape=jax.ShapeDtypeStruct((members_dev, inner_cells), f32),
        grid_spec=pltpu.PrefetchScalarGridSpec(
            num_scalar_prefetch=1,
            grid=(inner_cells // block,),
            in_specs=[
                mine,
                mine,
                pl.BlockSpec((members_dev, block), lambda i, place: (0, i)),
                pl.BlockSpec((SAMPLE_TOTAL, block), lambda i, place: (0, i)),
            ],
            out_specs=pl.BlockSpec((members_dev, block), lambda i, place: (0, i)),
        ),
        compiler_params=pltpu.CompilerParams(vmem_limit_bytes=VMEM_LIMIT),
        cost_estimate=pl.CostEstimate(flops=3_000_000_000, bytes_accessed=10_000_000, transcendentals=0),
    )(me.reshape(1), high_part, low_part, inner, all_inner)
    new = call(
        join_kernel,
        jax.ShapeDtypeStruct((members_dev * tile_rows, width), f32),
        [pltpu.VMEM((members_dev * tile_rows * 4, 128), f32)],
    )(inner, new)
    return new.reshape(prior_samples.shape)


def solution(mesh):
    return jax.shard_map(
        body,
        mesh=mesh,
        in_specs=(P("mem", "cell", None), P(None, "cell", None), P(), P(), P(), P()),
        out_specs=P("mem", "cell", None),
        check_vma=False,
    )
```

```python
import functools

import jax
import jax.numpy as jnp
from jax import lax
from jax.experimental import pallas as pl
from jax.experimental.pallas import tpu as pltpu
from jax.sharding import PartitionSpec as P

SAMPLE_TOTAL = 512
NOBS = 128
ALL_OBS = 512
HIGHEST = lax.Precision.HIGHEST
NT = (((1,), (1,)), ((), ()))
TN = (((0,), (0,)), ((), ()))
NN = (((1,), (0,)), ((), ()))
LARGE = 60 * 1024 * 1024
MEDIUM = 20 * 1024 * 1024
SMALL = 8 * 1024 * 1024


def halves(value):
    high = value.astype(jnp.bfloat16)
    low = (value - high.astype(jnp.float32)).astype(jnp.bfloat16)
    return high, low


def dot_split(left, right, dims):
    f32 = jnp.float32
    left_high, left_low = left
    right_high, right_low = right
    small = lax.dot_general(left_low, right_high, dims, preferred_element_type=f32)
    small = small + lax.dot_general(left_high, right_low, dims, preferred_element_type=f32)
    return small + lax.dot_general(left_high, right_high, dims, preferred_element_type=f32)


def dot3(left, right, dims):
    return dot_split(halves(left), halves(right), dims)


def dot6(left, right, dims):
    return lax.dot_general(
        left, right, dims, precision=HIGHEST, preferred_element_type=jnp.float32
    )


def forecast_kernel(order_ref, base_ref, x_ref, weight_ref, cell_ref, piece_ref, own_ref, pick_ref, flat_ref):
    members, rows, width = x_ref.shape
    col_at = lax.broadcasted_iota(jnp.int32, (rows, width), 1)
    row_at = lax.broadcasted_iota(jnp.int32, (rows, width), 0)
    east, west, north, south = [weight_ref[i] for i in range(4)]
    cell = jnp.concatenate([cell_ref[pl.ds(order_ref[j], 1), :] for j in range(order_ref.shape[0])], axis=1)
    at_row = (cell >> 9) - base_ref[0]

    @pl.when(pl.program_id(0) == 0)
    def _():
        at_col = cell & (width - 1)
        pick = lax.broadcasted_iota(jnp.int32, (width, ALL_OBS), 0) == at_col
        pick_ref[...] = pick.astype(jnp.bfloat16)

    def member(m, carry):
        x = x_ref[m]
        to_east = jnp.where(col_at == width - 1, 0.0, pltpu.roll(x, width - 1, 1))
        to_west = jnp.where(col_at == 0, 0.0, pltpu.roll(x, 1, 1))
        to_north = jnp.where(row_at == 0, 0.0, pltpu.roll(x, 1, 0))
        to_south = jnp.where(row_at == rows - 1, 0.0, pltpu.roll(x, rows - 1, 0))
        f = (
            x
            + east * (to_east - x)
            + west * (to_west - x)
            + north * (to_north - x)
            + south * (to_south - x)
        )
        flat_ref[pl.ds(pl.multiple_of(m * rows, rows), rows), :] = f
        for h in range(2):
            for q in range(4):
                piece_ref[4 * h + q, m] = f[8 * h : 8 * h + 8, 128 * q : 128 * q + 128]
        return carry

    lax.fori_loop(0, members, member, 0, unroll=4)
    own_row = (lax.broadcasted_iota(jnp.int32, (rows, ALL_OBS), 0) == at_row).astype(jnp.float32)
    pick = pick_ref[...]
    part = 8
    for g in range(members // part):
        value = flat_ref[g * part * rows : (g + 1) * part * rows, :]
        total = picked(value, pick).reshape(part, rows, ALL_OBS) * own_row[None]
        own_ref[part * g : part * g + part, :] = jnp.sum(total, axis=1)


def picked(value, pick):
    total = None
    for _ in range(3):
        cut = value.astype(jnp.bfloat16)
        value = value - cut.astype(jnp.float32)
        term = lax.dot_general(cut, pick, NN, preferred_element_type=jnp.float32)
        total = term if total is None else total + term
    return total


def halo_kernel(order_ref, base_ref, own_ref, low_ref, high_ref, weight_ref, cell_ref, out_ref):
    members, width = low_ref.shape
    rows = weight_ref.shape[1]
    cell = jnp.concatenate([cell_ref[pl.ds(order_ref[j], 1), :] for j in range(order_ref.shape[0])], axis=1)
    at_row = (cell >> 9) - base_ref[0]
    pick = lax.broadcasted_iota(jnp.int32, (width, ALL_OBS), 0) == (cell & (width - 1))
    edges = [low_ref[...], high_ref[...], weight_ref[2, 0:8, :], weight_ref[3, rows - 8 :, :]]
    edges = picked(jnp.concatenate(edges, axis=0), pick.astype(jnp.bfloat16))
    first = edges[2 * members : 2 * members + 1] * edges[0:members]
    last = edges[2 * members + 15 : 2 * members + 16] * edges[members : 2 * members]
    out_ref[...] = own_ref[...] + jnp.where(at_row == 0, first, 0.0) + jnp.where(at_row == rows - 1, last, 0.0)


def edge_kernel(piece_ref, weight_ref, low_ref, high_ref, out_ref):
    members = low_ref.shape[0]
    rows = weight_ref.shape[1]
    out_ref[...] = piece_ref[...]

    @pl.when(pl.program_id(0) < 4)
    def _():
        at = pl.ds(0, members, stride=8)
        out_ref[at, :] = out_ref[at, :] + weight_ref[2, 0:1, :] * low_ref[...]

    @pl.when(pl.program_id(0) >= 4)
    def _():
        at = pl.ds(7, members, stride=8)
        out_ref[at, :] = out_ref[at, :] + weight_ref[3, rows - 1 : rows, :] * high_ref[...]


def sum_kernel(*refs):
    total = refs[0][...]
    for ref in refs[1:-1]:
        total = total + ref[...]
    refs[-1][...] = total


def over_rows(value, row):
    return jnp.broadcast_to(value[row : row + 1, :], (8, NOBS))


def over_lanes(value, lane):
    return jnp.broadcast_to(value[:, lane : lane + 1], (8, NOBS))


def factor(block, root):
    count = NOBS // 8
    sub = lax.broadcasted_iota(jnp.int32, (8, NOBS), 0)
    lane = lax.broadcasted_iota(jnp.int32, (8, NOBS), 1)
    rows = [block[8 * i : 8 * i + 8, :] for i in range(count)]
    shifted = [(lane == sub + 8 * i).astype(jnp.float32) for i in range(count)]
    inverse = [None] * count
    for b in range(count):
        panel = rows[b]
        column = [over_lanes(panel, 8 * b + k) for k in range(8)]
        done = jnp.zeros((8, NOBS), jnp.float32)
        plus = shifted[b]
        inv_roots = []
        for k in range(8):
            at = 8 * b + k
            pivot = over_rows(column[k], k)
            inv_root = lax.rsqrt(pivot)
            inv = inv_root * inv_root
            inv_roots.append(inv_root)
            row = jnp.where(lane == at, 1.0, over_rows(panel, k))
            done = jnp.where(sub == k, row * inv_root, done)
            scaled = row * inv
            away = jnp.where(sub == k, -1.0, column[k])
            panel = jnp.where((sub == k) | (lane == at), 0.0, panel) - away * scaled
            plus_row = over_rows(plus, k) / (pivot * inv_root + over_rows(root[8 * b : 8 * b + 8, :], k))
            below = jnp.where(sub > k, column[k] * inv_root, 0.0)
            plus = jnp.where(sub == k, plus_row, plus - below * plus_row)
            for j in range(k + 1, 8):
                step = over_rows(column[j], k) * inv
                column[j] = jnp.where(sub == k, 0.0, column[j]) - away * step
        inverse[b] = jnp.where(lane <= sub + 8 * b, done, 0.0)
        shifted[b] = plus
        if b == count - 1:
            break
        for k in reversed(range(8)):
            above = jnp.where(sub < k, over_lanes(done, 8 * b + k), 0.0)
            row = over_rows(plus, k) * inv_roots[k]
            plus = jnp.where(sub == k, row, plus - above * row)
        panel_rows = [over_rows(panel, k) for k in range(8)]
        plus_rows = [over_rows(plus, k) for k in range(8)]
        inside = (lane >= 8 * b) & (lane < 8 * b + 8)
        for r in range(b + 1, count):
            left = [over_lanes(rows[r], 8 * b + k) for k in range(8)]
            new = jnp.where(inside, 0.0, rows[r])
            new_shifted = shifted[r]
            for k in range(8):
                new = new - left[k] * panel_rows[k]
                new_shifted = new_shifted - left[k] * plus_rows[k]
            rows[r] = new
            shifted[r] = new_shifted
    return jnp.concatenate(inverse, axis=0), jnp.concatenate(shifted, axis=0)


def transform_kernel(
    block_ref, me_ref, seen_ref, other_ref, value_ref, var_ref,
    out_ref, cov_ref, state_ref, gain_ref, minus_ref,
):
    n = ALL_OBS
    blocks = n // NOBS
    turns, share = seen_ref.shape[0], seen_ref.shape[1]
    value = jnp.concatenate([value_ref[pl.ds(block_ref[j], 1), :] for j in range(blocks)], axis=1)
    var = jnp.concatenate([var_ref[pl.ds(block_ref[j], 1), :] for j in range(blocks)], axis=1)
    total = seen_ref[0] + other_ref[0]
    for d in range(1, turns):
        total = total + seen_ref[d] + other_ref[d]
    mean = jnp.sum(total, axis=0, keepdims=True) / SAMPLE_TOTAL

    me = me_ref[0]

    def at(turn, other):
        place = (me + 2 * (turns - turn)) & (2 * turns - 1)
        place = place ^ 1 if other else place
        return pl.ds(pl.multiple_of(place * share, share), share)

    for d in range(turns):
        state_ref[at(d, False), :] = seen_ref[d] - mean
        state_ref[at(d, True), :] = other_ref[d] - mean
    state_ref[SAMPLE_TOTAL:, :] = jnp.broadcast_to(value - mean, (8, n))
    anomaly = state_ref[0:SAMPLE_TOTAL, :]
    minus_ref[...] = anomaly
    cov = dot6(anomaly, anomaly, TN) / (SAMPLE_TOTAL - 1)
    eye = lax.broadcasted_iota(jnp.int32, (n, n), 0) == lax.broadcasted_iota(jnp.int32, (n, n), 1)
    cov_ref[...] = cov + jnp.where(eye, var, 0.0)
    for j in range(blocks):
        low, high = NOBS * j, NOBS * (j + 1)
        root = jnp.sqrt(jnp.broadcast_to(var[:, low:high], (NOBS, NOBS))).T
        inv_low, inv_sum = factor(cov_ref[low:high, low:high], root)
        rest = high < n
        if rest:
            below = dot6(cov_ref[high:, low:high], inv_low, NT)
            cov_ref[high:, high:] = cov_ref[high:, high:] - dot6(below, below, NT)
            below = halves(below)
        inv_low, inv_sum = halves(inv_low), halves(inv_sum)
        gain = dot_split(halves(state_ref[:, low:high]), inv_low, NT)
        minus = dot_split(halves(minus_ref[:, low:high]), inv_sum, NT)
        gain_ref[:, low:high] = gain
        if rest:
            state_ref[:, high:] = state_ref[:, high:] - dot_split(halves(gain), below, NT)
            minus_ref[:, high:] = minus_ref[:, high:] - dot_split(halves(minus), below, NT)
        minus_ref[:, low:high] = minus
    mean_step = gain_ref[SAMPLE_TOTAL : SAMPLE_TOTAL + 1, :]
    left = (mean_step - minus_ref[...]) * (1.0 / (SAMPLE_TOTAL - 1))
    total = dot3(left, gain_ref[0:SAMPLE_TOTAL, :], NT)
    out_ref[...] = total


def update_kernel(transform_ref, cells_ref, out_ref):
    transform = halves(transform_ref[...])
    for r in range(0, 8, 2):
        at = [pl.ds(r + i, SAMPLE_TOTAL, stride=8) for i in range(2)]
        field = jnp.concatenate([cells_ref[a, :] for a in at], axis=1)
        new = field + dot_split(transform, halves(field), NN)
        for i in range(2):
            out_ref[at[i], :] = new[:, 128 * i : 128 * i + 128]


def stack_kernel(*refs):
    for i, ref in enumerate(refs[:-1]):
        refs[-1][i] = ref[...]


def join_kernel(parts_ref, out_ref):
    for h in range(2):
        for q in range(4):
            out_ref[:, 8 * h : 8 * h + 8, 128 * q : 128 * q + 128] = parts_ref[4 * h + q]


def call(kernel, out_shape, scratch=(), grid=(), scalars=0, in_specs=None, out_specs=None, flops=0, bytes_accessed=0, limit=MEDIUM):
    specs = {} if in_specs is None else {"in_specs": in_specs, "out_specs": out_specs}
    return pl.pallas_call(
        kernel,
        out_shape=out_shape,
        grid_spec=pltpu.PrefetchScalarGridSpec(
            num_scalar_prefetch=scalars, grid=grid, scratch_shapes=list(scratch), **specs
        ),
        compiler_params=pltpu.CompilerParams(vmem_limit_bytes=limit),
        cost_estimate=pl.CostEstimate(flops=flops, bytes_accessed=bytes_accessed, transcendentals=0),
    )


def spec(shape, *axes):
    places = tuple(axes) + (None,) * (len(shape) - len(axes))
    return pl.BlockSpec(shape, lambda i, *scalars: tuple(0 if p is None else i for p in places))


def body(prior_samples, neighbour_weights, obs_cell, obs_value, obs_var, block_order):
    f32 = jnp.float32
    members, rows, width = prior_samples.shape
    mem_count, cell_count = lax.axis_size("mem"), lax.axis_size("cell")
    me = lax.axis_index("mem")
    base = (lax.axis_index("cell") * rows).reshape(1)
    shape = jax.ShapeDtypeStruct
    steps = 4
    step = members // steps
    side = 4
    forward = [(i, i + 1) for i in range(cell_count - 1)]
    backward = [(i + 1, i) for i in range(cell_count - 1)]
    swap = [(i, i ^ 1) for i in range(mem_count)]

    def along_x(value, d):
        return lax.ppermute(value, "mem", [(i, (i + 2 * d) % mem_count) for i in range(mem_count)])

    near, far = [1, 0, 3, 2], [3, 2, 1, 0]
    z_near, z_far = [[(i, i // side * side + p[i % side]) for i in range(cell_count)] for p in (near, far)]
    y_near, y_far = [[(i, p[i // side] * side + i % side) for i in range(cell_count)] for p in (near, far)]

    low = lax.ppermute(prior_samples[:, rows - 1, :], "cell", forward)
    high = lax.ppermute(prior_samples[:, 0, :], "cell", backward)
    smem = pl.BlockSpec(memory_space=pltpu.SMEM)
    seen_shape = shape((members, ALL_OBS), f32)
    pieces, seen = call(
        forecast_kernel,
        (shape((mem_count, members, 8, 128), f32), seen_shape),
        [
            pltpu.VMEM((width, ALL_OBS), jnp.bfloat16),
            pltpu.VMEM((step * rows, width), f32),
        ],
        grid=(steps,),
        in_specs=[
            smem,
            smem,
            spec((step, rows, width), 0),
            spec((4, rows, width)),
            spec(obs_cell.shape),
        ],
        out_specs=[spec((mem_count, step, 8, 128), None, 0), spec((step, ALL_OBS), 0)],
        flops=2_000_000_000,
        bytes_accessed=4_000_000,
        limit=LARGE,
    )(block_order, base, prior_samples, neighbour_weights, obs_cell)
    seen = call(
        halo_kernel,
        seen_shape,
        in_specs=[smem, smem] + [pl.BlockSpec(memory_space=pltpu.VMEM)] * 5,
        out_specs=pl.BlockSpec(memory_space=pltpu.VMEM),
        limit=SMALL,
    )(block_order, base, seen, low, high, neighbour_weights, obs_cell)

    for pairs in (z_near, z_far, y_near, y_far):
        seen = call(sum_kernel, seen_shape, limit=SMALL)(seen, lax.ppermute(seen, "cell", pairs))
    lanes = pl.BlockSpec((members, 128), lambda i: (0, i % 4))
    tiles = spec((members * 8, 128), 0)
    pieces = pl.pallas_call(
        edge_kernel,
        out_shape=shape((mem_count * members * 8, 128), f32),
        grid=(mem_count,),
        in_specs=[tiles, pl.BlockSpec((4, rows, 128), lambda i: (0, 0, i % 4)), lanes, lanes],
        out_specs=tiles,
        input_output_aliases={0: 0},
        compiler_params=pltpu.CompilerParams(vmem_limit_bytes=SMALL),
    )(pieces.reshape(mem_count * members * 8, 128), neighbour_weights, low, high)
    pieces = pieces.reshape(mem_count, members, 8, 128)
    one, two, three = along_x(seen, 1), along_x(seen, 2), along_x(seen, 3)
    one, two, three, pieces = lax.optimization_barrier((one, two, three, pieces))
    cells = lax.all_to_all(pieces, "mem", 0, 0)
    seen = call(stack_kernel, shape((4, members, ALL_OBS), f32), limit=SMALL)(seen, one, two, three)
    other = lax.ppermute(seen, "mem", swap)

    square = (ALL_OBS, ALL_OBS)
    whole = pl.BlockSpec(memory_space=pltpu.VMEM)
    transform = call(
        transform_kernel,
        shape(square, f32),
        [
            pltpu.VMEM(square, f32),
            pltpu.VMEM((SAMPLE_TOTAL + 8, ALL_OBS), f32),
            pltpu.VMEM((SAMPLE_TOTAL + 8, ALL_OBS), f32),
            pltpu.VMEM(square, f32),
        ],
        scalars=2,
        in_specs=[whole] * 4,
        out_specs=whole,
        flops=20_000_000_000,
        bytes_accessed=2_000_000,
    )(block_order, me.reshape(1), seen, other, obs_value, obs_var)

    cells = cells.reshape(SAMPLE_TOTAL * 8, 128)
    new = call(update_kernel, shape(cells.shape, f32), flops=3_000_000_000, bytes_accessed=4_000_000)(
        transform, cells
    )
    new = lax.all_to_all(new.reshape(mem_count, members, 8, 128), "mem", 0, 0)
    return call(
        join_kernel,
        shape(prior_samples.shape, f32),
        grid=(4,),
        in_specs=[spec((mem_count, step, 8, 128), None, 0)],
        out_specs=spec((step, rows, width), 0),
        bytes_accessed=4_000_000,
    )(new)


def solution(mesh):
    return jax.shard_map(
        body,
        mesh=mesh,
        in_specs=(P("mem", "cell", None), P(None, "cell", None), P(), P(), P(), P()),
        out_specs=P("mem", "cell", None),
        check_vma=False,
    )
```

```python
import functools

import jax
import jax.numpy as jnp
from jax import lax
from jax.experimental import pallas as pl
from jax.experimental.pallas import tpu as pltpu
from jax.sharding import PartitionSpec as P

SAMPLE_TOTAL = 512
NOBS = 128
ALL_OBS = 512
HIGHEST = lax.Precision.HIGHEST
NT = (((1,), (1,)), ((), ()))
TN = (((0,), (0,)), ((), ()))
NN = (((1,), (0,)), ((), ()))
LARGE = 60 * 1024 * 1024
MEDIUM = 20 * 1024 * 1024
SMALL = 8 * 1024 * 1024


def halves(value):
    high = value.astype(jnp.bfloat16)
    low = (value - high.astype(jnp.float32)).astype(jnp.bfloat16)
    return high, low


def dot_split(left, right, dims):
    f32 = jnp.float32
    left_high, left_low = left
    right_high, right_low = right
    small = lax.dot_general(left_low, right_high, dims, preferred_element_type=f32)
    small = small + lax.dot_general(left_high, right_low, dims, preferred_element_type=f32)
    return small + lax.dot_general(left_high, right_high, dims, preferred_element_type=f32)


def dot3(left, right, dims):
    return dot_split(halves(left), halves(right), dims)


def dot6(left, right, dims):
    return lax.dot_general(
        left, right, dims, precision=HIGHEST, preferred_element_type=jnp.float32
    )


def forecast_kernel(order_ref, base_ref, x_ref, weight_ref, cell_ref, piece_ref, own_ref, pick_ref, flat_ref):
    members, rows, width = x_ref.shape
    col_at = lax.broadcasted_iota(jnp.int32, (rows, width), 1)
    row_at = lax.broadcasted_iota(jnp.int32, (rows, width), 0)
    east, west, north, south = [weight_ref[i] for i in range(4)]
    cell = jnp.concatenate([cell_ref[pl.ds(order_ref[j], 1), :] for j in range(order_ref.shape[0])], axis=1)
    at_row = (cell >> 9) - base_ref[0]

    @pl.when(pl.program_id(0) == 0)
    def _():
        at_col = cell & (width - 1)
        pick = lax.broadcasted_iota(jnp.int32, (width, ALL_OBS), 0) == at_col
        pick_ref[...] = pick.astype(jnp.bfloat16)

    def member(m, carry):
        x = x_ref[m]
        to_east = jnp.where(col_at == width - 1, 0.0, pltpu.roll(x, width - 1, 1))
        to_west = jnp.where(col_at == 0, 0.0, pltpu.roll(x, 1, 1))
        to_north = jnp.where(row_at == 0, 0.0, pltpu.roll(x, 1, 0))
        to_south = jnp.where(row_at == rows - 1, 0.0, pltpu.roll(x, rows - 1, 0))
        f = (
            x
            + east * (to_east - x)
            + west * (to_west - x)
            + north * (to_north - x)
            + south * (to_south - x)
        )
        flat_ref[pl.ds(pl.multiple_of(m * rows, rows), rows), :] = f
        for h in range(2):
            for q in range(4):
                piece_ref[4 * h + q, m] = f[8 * h : 8 * h + 8, 128 * q : 128 * q + 128]
        return carry

    lax.fori_loop(0, members, member, 0, unroll=4)
    own_row = (lax.broadcasted_iota(jnp.int32, (rows, ALL_OBS), 0) == at_row).astype(jnp.float32)
    pick = pick_ref[...]
    part = 8
    for g in range(members // part):
        value = flat_ref[g * part * rows : (g + 1) * part * rows, :]
        total = picked(value, pick).reshape(part, rows, ALL_OBS) * own_row[None]
        own_ref[part * g : part * g + part, :] = jnp.sum(total, axis=1)


def picked(value, pick):
    total = None
    for _ in range(3):
        cut = value.astype(jnp.bfloat16)
        value = value - cut.astype(jnp.float32)
        term = lax.dot_general(cut, pick, NN, preferred_element_type=jnp.float32)
        total = term if total is None else total + term
    return total


def halo_kernel(order_ref, base_ref, own_ref, low_ref, high_ref, weight_ref, cell_ref, out_ref):
    members, width = low_ref.shape
    rows = weight_ref.shape[1]
    cell = jnp.concatenate([cell_ref[pl.ds(order_ref[j], 1), :] for j in range(order_ref.shape[0])], axis=1)
    at_row = (cell >> 9) - base_ref[0]
    pick = lax.broadcasted_iota(jnp.int32, (width, ALL_OBS), 0) == (cell & (width - 1))
    edges = [low_ref[...], high_ref[...], weight_ref[2, 0:8, :], weight_ref[3, rows - 8 :, :]]
    edges = picked(jnp.concatenate(edges, axis=0), pick.astype(jnp.bfloat16))
    first = edges[2 * members : 2 * members + 1] * edges[0:members]
    last = edges[2 * members + 15 : 2 * members + 16] * edges[members : 2 * members]
    out_ref[...] = own_ref[...] + jnp.where(at_row == 0, first, 0.0) + jnp.where(at_row == rows - 1, last, 0.0)


def edge_kernel(piece_ref, weight_ref, low_ref, high_ref, out_ref):
    members = low_ref.shape[0]
    rows = weight_ref.shape[1]
    upper = pl.program_id(0) == 0
    out_ref[...] = piece_ref[...]
    weight = jnp.where(upper, weight_ref[2, 0:1, :], weight_ref[3, rows - 1 : rows, :])
    change = weight * jnp.where(upper, low_ref[...], high_ref[...])

    def add(first):
        for q in range(4):
            at = pl.ds(members * 8 * q + first, members, stride=8)
            out_ref[at, :] = out_ref[at, :] + change[:, 128 * q : 128 * q + 128]

    pl.when(upper)(lambda: add(0))
    pl.when(jnp.logical_not(upper))(lambda: add(7))


def sum_kernel(*refs):
    total = refs[0][...]
    for ref in refs[1:-1]:
        total = total + ref[...]
    refs[-1][...] = total


def over_rows(value, row):
    return jnp.broadcast_to(value[row : row + 1, :], (8, NOBS))


def over_lanes(value, lane):
    return jnp.broadcast_to(value[:, lane : lane + 1], (8, NOBS))


def factor(block, root):
    count = NOBS // 8
    sub = lax.broadcasted_iota(jnp.int32, (8, NOBS), 0)
    lane = lax.broadcasted_iota(jnp.int32, (8, NOBS), 1)
    rows = [block[8 * i : 8 * i + 8, :] for i in range(count)]
    shifted = [(lane == sub + 8 * i).astype(jnp.float32) for i in range(count)]
    inverse = [None] * count
    for b in range(count):
        panel = rows[b]
        column = [over_lanes(panel, 8 * b + k) for k in range(8)]
        done = jnp.zeros((8, NOBS), jnp.float32)
        plus = shifted[b]
        inv_roots = []
        for k in range(8):
            at = 8 * b + k
            pivot = over_rows(column[k], k)
            inv_root = lax.rsqrt(pivot)
            inv = pl.reciprocal(pivot)
            inv_roots.append(inv_root)
            row = jnp.where(lane == at, 1.0, over_rows(panel, k))
            done = jnp.where(sub == k, row * inv_root, done)
            away = jnp.where(sub == k, -1.0, column[k])
            panel = jnp.where((sub == k) | (lane == at), 0.0, panel) - (away * row) * inv
            plus_row = over_rows(plus, k) / (pivot * inv_root + over_rows(root[8 * b : 8 * b + 8, :], k))
            below = jnp.where(sub > k, column[k] * inv_root, 0.0)
            plus = jnp.where(sub == k, plus_row, plus - below * plus_row)
            for j in range(k + 1, 8):
                step = away * over_rows(column[j], k)
                column[j] = jnp.where(sub == k, 0.0, column[j]) - step * inv
        inverse[b] = jnp.where(lane <= sub + 8 * b, done, 0.0)
        shifted[b] = plus
        if b == count - 1:
            break
        for k in reversed(range(8)):
            above = jnp.where(sub < k, over_lanes(done, 8 * b + k), 0.0)
            row = over_rows(plus, k) * inv_roots[k]
            plus = jnp.where(sub == k, row, plus - above * row)
        panel_rows = [over_rows(panel, k) for k in range(8)]
        plus_rows = [over_rows(plus, k) for k in range(8)]
        inside = (lane >= 8 * b) & (lane < 8 * b + 8)
        for r in range(b + 1, count):
            left = [over_lanes(rows[r], 8 * b + k) for k in range(8)]
            new = jnp.where(inside, 0.0, rows[r])
            new_shifted = shifted[r]
            for k in range(8):
                new = new - left[k] * panel_rows[k]
                new_shifted = new_shifted - left[k] * plus_rows[k]
            rows[r] = new
            shifted[r] = new_shifted
    return jnp.concatenate(inverse, axis=0), jnp.concatenate(shifted, axis=0)


def transform_kernel(
    block_ref, me_ref, seen_ref, other_ref, value_ref, var_ref,
    out_ref, cov_ref, state_ref, gain_ref, minus_ref,
):
    n = ALL_OBS
    blocks = n // NOBS
    turns, share = seen_ref.shape[0], seen_ref.shape[1]
    value = jnp.concatenate([value_ref[pl.ds(block_ref[j], 1), :] for j in range(blocks)], axis=1)
    var = jnp.concatenate([var_ref[pl.ds(block_ref[j], 1), :] for j in range(blocks)], axis=1)
    total = seen_ref[0] + other_ref[0]
    for d in range(1, turns):
        total = total + seen_ref[d] + other_ref[d]
    mean = jnp.sum(total, axis=0, keepdims=True) / SAMPLE_TOTAL

    me = me_ref[0]

    def at(turn, other):
        place = (me + 2 * (turns - turn)) & (2 * turns - 1)
        place = place ^ 1 if other else place
        return pl.ds(pl.multiple_of(place * share, share), share)

    for d in range(turns):
        state_ref[at(d, False), :] = seen_ref[d] - mean
        state_ref[at(d, True), :] = other_ref[d] - mean
    state_ref[SAMPLE_TOTAL:, :] = jnp.broadcast_to(value - mean, (8, n))
    anomaly = state_ref[0:SAMPLE_TOTAL, :]
    minus_ref[...] = anomaly
    eye = lax.broadcasted_iota(jnp.int32, (NOBS, NOBS), 0) == lax.broadcasted_iota(jnp.int32, (NOBS, NOBS), 1)
    for j in range(blocks):
        low, high = NOBS * j, NOBS * (j + 1)
        cov = dot6(anomaly[:, low:], anomaly[:, low:high], TN) / (SAMPLE_TOTAL - 1)
        cov_ref[low:high, low:high] = cov[:NOBS] + jnp.where(eye, var[:, low:high], 0.0)
        if high < n:
            cov_ref[high:, low:high] = cov[NOBS:]
    for j in range(blocks):
        low, high = NOBS * j, NOBS * (j + 1)
        root = jnp.sqrt(jnp.broadcast_to(var[:, low:high], (NOBS, NOBS))).T
        inv_low, inv_sum = factor(cov_ref[low:high, low:high], root)
        rest = high < n
        if rest:
            below = dot6(cov_ref[high:, low:high], inv_low, NT)
            for at in range(high, n, NOBS):
                change = dot6(below[at - high :], below[at - high : at - high + NOBS], NT)
                cov_ref[at:, at : at + NOBS] = cov_ref[at:, at : at + NOBS] - change
            below = halves(below)
        inv_low, inv_sum = halves(inv_low), halves(inv_sum)
        gain = dot_split(halves(state_ref[:, low:high]), inv_low, NT)
        minus = dot_split(halves(minus_ref[:, low:high]), inv_sum, NT)
        gain_ref[:, low:high] = gain
        if rest:
            state_ref[:, high:] = state_ref[:, high:] - dot_split(halves(gain), below, NT)
            minus_ref[:, high:] = minus_ref[:, high:] - dot_split(halves(minus), below, NT)
        minus_ref[:, low:high] = minus
    mean_step = gain_ref[SAMPLE_TOTAL : SAMPLE_TOTAL + 1, :]
    left = (mean_step - minus_ref[...]) * (1.0 / (SAMPLE_TOTAL - 1))
    total = dot3(left, gain_ref[0:SAMPLE_TOTAL, :], NT)
    out_ref[...] = total


def update_kernel(transform_ref, cells_ref, out_ref):
    transform = halves(transform_ref[...])
    for r in range(0, 8, 2):
        at = [pl.ds(r + i, SAMPLE_TOTAL, stride=8) for i in range(2)]
        field = jnp.concatenate([cells_ref[a, :] for a in at], axis=1)
        new = field + dot_split(transform, halves(field), NN)
        for i in range(2):
            out_ref[at[i], :] = new[:, 128 * i : 128 * i + 128]


def stack_kernel(*refs):
    for i, ref in enumerate(refs[:-1]):
        refs[-1][i] = ref[...]


def join_kernel(parts_ref, out_ref):
    for h in range(2):
        for q in range(4):
            out_ref[:, 8 * h : 8 * h + 8, 128 * q : 128 * q + 128] = parts_ref[4 * h + q]


def call(kernel, out_shape, scratch=(), grid=(), scalars=0, in_specs=None, out_specs=None, flops=0, bytes_accessed=0, limit=MEDIUM):
    specs = {} if in_specs is None else {"in_specs": in_specs, "out_specs": out_specs}
    return pl.pallas_call(
        kernel,
        out_shape=out_shape,
        grid_spec=pltpu.PrefetchScalarGridSpec(
            num_scalar_prefetch=scalars, grid=grid, scratch_shapes=list(scratch), **specs
        ),
        compiler_params=pltpu.CompilerParams(vmem_limit_bytes=limit),
        cost_estimate=pl.CostEstimate(flops=flops, bytes_accessed=bytes_accessed, transcendentals=0),
    )


def spec(shape, *axes):
    places = tuple(axes) + (None,) * (len(shape) - len(axes))
    return pl.BlockSpec(shape, lambda i, *scalars: tuple(0 if p is None else i for p in places))


def body(prior_samples, neighbour_weights, obs_cell, obs_value, obs_var, block_order):
    f32 = jnp.float32
    members, rows, width = prior_samples.shape
    mem_count, cell_count = lax.axis_size("mem"), lax.axis_size("cell")
    me = lax.axis_index("mem")
    base = (lax.axis_index("cell") * rows).reshape(1)
    shape = jax.ShapeDtypeStruct
    steps = 4
    step = members // steps
    side = 4
    forward = [(i, i + 1) for i in range(cell_count - 1)]
    backward = [(i + 1, i) for i in range(cell_count - 1)]
    swap = [(i, i ^ 1) for i in range(mem_count)]

    def along_x(value, d):
        return lax.ppermute(value, "mem", [(i, (i + 2 * d) % mem_count) for i in range(mem_count)])

    def ring(value, phase, d):
        def target(m, i):
            z, y = i % side, i // side
            if (m + phase) % 2 == 0:
                z = (z + d) % side
            else:
                y = (y + d) % side
            return m * cell_count + y * side + z

        places = [(m, i) for m in range(mem_count) for i in range(cell_count)]
        return lax.ppermute(value, ("mem", "cell"), [(m * cell_count + i, target(m, i)) for m, i in places])

    low = lax.ppermute(prior_samples[:, rows - 1, :], "cell", forward)
    high = lax.ppermute(prior_samples[:, 0, :], "cell", backward)
    smem = pl.BlockSpec(memory_space=pltpu.SMEM)
    seen_shape = shape((members, ALL_OBS), f32)
    pieces, seen = call(
        forecast_kernel,
        (shape((mem_count, members, 8, 128), f32), seen_shape),
        [
            pltpu.VMEM((width, ALL_OBS), jnp.bfloat16),
            pltpu.VMEM((step * rows, width), f32),
        ],
        grid=(steps,),
        in_specs=[
            smem,
            smem,
            spec((step, rows, width), 0),
            spec((4, rows, width)),
            spec(obs_cell.shape),
        ],
        out_specs=[spec((mem_count, step, 8, 128), None, 0), spec((step, ALL_OBS), 0)],
        flops=2_000_000_000,
        bytes_accessed=4_000_000,
        limit=LARGE,
    )(block_order, base, prior_samples, neighbour_weights, obs_cell)
    seen = call(
        halo_kernel,
        seen_shape,
        grid=(1,),
        in_specs=[
            smem,
            smem,
            spec((members, ALL_OBS)),
            spec((members, width)),
            spec((members, width)),
            spec((4, rows, width)),
            spec(obs_cell.shape),
        ],
        out_specs=spec((members, ALL_OBS)),
        limit=SMALL,
    )(block_order, base, seen, low, high, neighbour_weights, obs_cell)

    tiles = spec((4 * members * 8, 128), 0)
    pieces = pl.pallas_call(
        edge_kernel,
        out_shape=shape((mem_count * members * 8, 128), f32),
        grid=(2,),
        in_specs=[tiles, spec((4, rows, width)), spec((members, width)), spec((members, width))],
        out_specs=tiles,
        input_output_aliases={0: 0},
        compiler_params=pltpu.CompilerParams(vmem_limit_bytes=MEDIUM),
    )(pieces.reshape(mem_count * members * 8, 128), neighbour_weights, low, high)
    pieces = pieces.reshape(mem_count, members, 8, 128)

    for phase in range(2):
        others = [ring(seen, phase, d) for d in (2, 1, 3)]
        if phase == 0:
            pieces, *others = lax.optimization_barrier([pieces] + others)
        seen = call(sum_kernel, seen_shape, limit=SMALL)(seen, *others)
    one, two, three = along_x(seen, 1), along_x(seen, 2), along_x(seen, 3)
    one, two, three, pieces = lax.optimization_barrier((one, two, three, pieces))
    cells = lax.all_to_all(pieces, "mem", 0, 0)
    seen = call(stack_kernel, shape((4, members, ALL_OBS), f32), limit=SMALL)(seen, one, two, three)
    other = lax.ppermute(seen, "mem", swap)

    square = (ALL_OBS, ALL_OBS)
    transform = call(
        transform_kernel,
        shape(square, f32),
        [
            pltpu.VMEM(square, f32),
            pltpu.VMEM((SAMPLE_TOTAL + 8, ALL_OBS), f32),
            pltpu.VMEM((SAMPLE_TOTAL + 8, ALL_OBS), f32),
            pltpu.VMEM(square, f32),
        ],
        grid=(1,),
        scalars=2,
        in_specs=[
            spec((4, members, ALL_OBS)),
            spec((4, members, ALL_OBS)),
            spec(obs_value.shape),
            spec(obs_var.shape),
        ],
        out_specs=spec(square),
        flops=20_000_000_000,
        bytes_accessed=2_000_000,
    )(block_order, me.reshape(1), seen, other, obs_value, obs_var)

    cells = cells.reshape(SAMPLE_TOTAL * 8, 128)
    new = call(update_kernel, shape(cells.shape, f32), flops=3_000_000_000, bytes_accessed=4_000_000)(
        transform, cells
    )
    new = lax.all_to_all(new.reshape(mem_count, members, 8, 128), "mem", 0, 0)
    return call(
        join_kernel,
        shape(prior_samples.shape, f32),
        grid=(4,),
        in_specs=[spec((mem_count, step, 8, 128), None, 0)],
        out_specs=spec((step, rows, width), 0),
        bytes_accessed=4_000_000,
    )(new)


def solution(mesh):
    return jax.shard_map(
        body,
        mesh=mesh,
        in_specs=(P("mem", "cell", None), P(None, "cell", None), P(), P(), P(), P()),
        out_specs=P("mem", "cell", None),
        check_vma=False,
    )
```

```python
import functools

import jax
import jax.numpy as jnp
from jax import lax
from jax.experimental import pallas as pl
from jax.experimental.pallas import tpu as pltpu
from jax.sharding import PartitionSpec as P

SAMPLE_TOTAL = 512
NOBS = 128
ALL_OBS = 512
HIGHEST = lax.Precision.HIGHEST
NT = (((1,), (1,)), ((), ()))
TN = (((0,), (0,)), ((), ()))
NN = (((1,), (0,)), ((), ()))
LARGE = 60 * 1024 * 1024
MEDIUM = 20 * 1024 * 1024
SMALL = 8 * 1024 * 1024


def halves(value):
    high = value.astype(jnp.bfloat16)
    low = (value - high.astype(jnp.float32)).astype(jnp.bfloat16)
    return high, low


def dot_split(left, right, dims):
    f32 = jnp.float32
    left_high, left_low = left
    right_high, right_low = right
    small = lax.dot_general(left_low, right_high, dims, preferred_element_type=f32)
    small = small + lax.dot_general(left_high, right_low, dims, preferred_element_type=f32)
    return small + lax.dot_general(left_high, right_high, dims, preferred_element_type=f32)


def dot3(left, right, dims):
    return dot_split(halves(left), halves(right), dims)


def dot6(left, right, dims):
    return lax.dot_general(
        left, right, dims, precision=HIGHEST, preferred_element_type=jnp.float32
    )


def forecast_kernel(order_ref, base_ref, x_ref, weight_ref, cell_ref, piece_ref, own_ref, pick_ref, flat_ref):
    members, rows, width = x_ref.shape
    col_at = lax.broadcasted_iota(jnp.int32, (rows, width), 1)
    row_at = lax.broadcasted_iota(jnp.int32, (rows, width), 0)
    east, west, north, south = [weight_ref[i] for i in range(4)]
    cell = jnp.concatenate([cell_ref[pl.ds(order_ref[j], 1), :] for j in range(order_ref.shape[0])], axis=1)
    at_row = (cell >> 9) - base_ref[0]

    @pl.when(pl.program_id(0) == 0)
    def _():
        at_col = cell & (width - 1)
        pick = lax.broadcasted_iota(jnp.int32, (width, ALL_OBS), 0) == at_col
        pick_ref[...] = pick.astype(jnp.bfloat16)

    def member(m, carry):
        x = x_ref[m]
        to_east = jnp.where(col_at == width - 1, 0.0, pltpu.roll(x, width - 1, 1))
        to_west = jnp.where(col_at == 0, 0.0, pltpu.roll(x, 1, 1))
        to_north = jnp.where(row_at == 0, 0.0, pltpu.roll(x, 1, 0))
        to_south = jnp.where(row_at == rows - 1, 0.0, pltpu.roll(x, rows - 1, 0))
        f = (
            x
            + east * (to_east - x)
            + west * (to_west - x)
            + north * (to_north - x)
            + south * (to_south - x)
        )
        flat_ref[pl.ds(pl.multiple_of(m * rows, rows), rows), :] = f
        for h in range(2):
            for q in range(4):
                piece_ref[4 * h + q, m] = f[8 * h : 8 * h + 8, 128 * q : 128 * q + 128]
        return carry

    lax.fori_loop(0, members, member, 0, unroll=8)
    own_row = (lax.broadcasted_iota(jnp.int32, (rows, ALL_OBS), 0) == at_row).astype(jnp.float32)
    pick = pick_ref[...]
    part = 8
    for g in range(members // part):
        value = flat_ref[g * part * rows : (g + 1) * part * rows, :]
        total = picked(value, pick).reshape(part, rows, ALL_OBS) * own_row[None]
        own_ref[part * g : part * g + part, :] = jnp.sum(total, axis=1)


def picked(value, pick):
    total = None
    for _ in range(3):
        cut = value.astype(jnp.bfloat16)
        value = value - cut.astype(jnp.float32)
        term = lax.dot_general(cut, pick, NN, preferred_element_type=jnp.float32)
        total = term if total is None else total + term
    return total


def halo_kernel(order_ref, base_ref, own_ref, low_ref, high_ref, weight_ref, cell_ref, out_ref):
    members, width = low_ref.shape
    rows = weight_ref.shape[1]
    cell = jnp.concatenate([cell_ref[pl.ds(order_ref[j], 1), :] for j in range(order_ref.shape[0])], axis=1)
    at_row = (cell >> 9) - base_ref[0]
    pick = lax.broadcasted_iota(jnp.int32, (width, ALL_OBS), 0) == (cell & (width - 1))
    edges = [low_ref[...], high_ref[...], weight_ref[2, 0:8, :], weight_ref[3, rows - 8 :, :]]
    edges = picked(jnp.concatenate(edges, axis=0), pick.astype(jnp.bfloat16))
    first = edges[2 * members : 2 * members + 1] * edges[0:members]
    last = edges[2 * members + 15 : 2 * members + 16] * edges[members : 2 * members]
    out_ref[...] = own_ref[...] + jnp.where(at_row == 0, first, 0.0) + jnp.where(at_row == rows - 1, last, 0.0)


def edge_kernel(piece_ref, weight_ref, low_ref, high_ref, out_ref):
    members = low_ref.shape[0]
    rows = weight_ref.shape[1]
    upper = pl.program_id(0) == 0
    out_ref[...] = piece_ref[...]
    weight = jnp.where(upper, weight_ref[2, 0:1, :], weight_ref[3, rows - 1 : rows, :])
    change = weight * jnp.where(upper, low_ref[...], high_ref[...])

    def add(first):
        for q in range(4):
            at = pl.ds(members * 8 * q + first, members, stride=8)
            out_ref[at, :] = out_ref[at, :] + change[:, 128 * q : 128 * q + 128]

    pl.when(upper)(lambda: add(0))
    pl.when(jnp.logical_not(upper))(lambda: add(7))


def sum_kernel(*refs):
    total = refs[0][...]
    for ref in refs[1:-1]:
        total = total + ref[...]
    refs[-1][...] = total


def over_rows(value, row):
    return jnp.broadcast_to(value[row : row + 1, :], (8, NOBS))


def over_lanes(value, lane):
    return jnp.broadcast_to(value[:, lane : lane + 1], (8, NOBS))


def factor(block, root):
    count = NOBS // 8
    sub = lax.broadcasted_iota(jnp.int32, (8, NOBS), 0)
    lane = lax.broadcasted_iota(jnp.int32, (8, NOBS), 1)
    rows = [block[8 * i : 8 * i + 8, :] for i in range(count)]
    shifted = [(lane == sub + 8 * i).astype(jnp.float32) for i in range(count)]
    inverse = [None] * count
    for b in range(count):
        panel = rows[b]
        column = [over_lanes(panel, 8 * b + k) for k in range(8)]
        done = jnp.zeros((8, NOBS), jnp.float32)
        plus = shifted[b]
        inv_roots = []
        for k in range(8):
            at = 8 * b + k
            pivot = over_rows(column[k], k)
            inv_root = lax.rsqrt(pivot)
            inv = pl.reciprocal(pivot)
            inv_roots.append(inv_root)
            row = jnp.where(lane == at, 1.0, over_rows(panel, k))
            done = jnp.where(sub == k, row * inv_root, done)
            away = jnp.where(sub == k, -1.0, column[k])
            panel = jnp.where((sub == k) | (lane == at), 0.0, panel) - (away * row) * inv
            plus_row = over_rows(plus, k) / (pivot * inv_root + over_rows(root[8 * b : 8 * b + 8, :], k))
            below = jnp.where(sub > k, column[k] * inv_root, 0.0)
            plus = jnp.where(sub == k, plus_row, plus - below * plus_row)
            for j in range(k + 1, 8):
                step = away * over_rows(column[j], k)
                column[j] = jnp.where(sub == k, 0.0, column[j]) - step * inv
        inverse[b] = jnp.where(lane <= sub + 8 * b, done, 0.0)
        shifted[b] = plus
        if b == count - 1:
            break
        for k in reversed(range(8)):
            above = jnp.where(sub < k, over_lanes(done, 8 * b + k), 0.0)
            row = over_rows(plus, k) * inv_roots[k]
            plus = jnp.where(sub == k, row, plus - above * row)
        panel_rows = [over_rows(panel, k) for k in range(8)]
        plus_rows = [over_rows(plus, k) for k in range(8)]
        inside = (lane >= 8 * b) & (lane < 8 * b + 8)
        for r in range(b + 1, count):
            left = [over_lanes(rows[r], 8 * b + k) for k in range(8)]
            new = jnp.where(inside, 0.0, rows[r])
            new_shifted = shifted[r]
            for k in range(8):
                new = new - left[k] * panel_rows[k]
                new_shifted = new_shifted - left[k] * plus_rows[k]
            rows[r] = new
            shifted[r] = new_shifted
    return jnp.concatenate(inverse, axis=0), jnp.concatenate(shifted, axis=0)


def transform_kernel(
    block_ref, me_ref, seen_ref, other_ref, value_ref, var_ref,
    out_ref, cov_ref, state_ref, gain_ref, minus_ref, total_ref,
):
    n = ALL_OBS
    blocks = n // NOBS
    turns, share = seen_ref.shape[0], seen_ref.shape[1]
    value = jnp.concatenate([value_ref[pl.ds(block_ref[j], 1), :] for j in range(blocks)], axis=1)
    var = jnp.concatenate([var_ref[pl.ds(block_ref[j], 1), :] for j in range(blocks)], axis=1)
    total = seen_ref[0] + other_ref[0]
    for d in range(1, turns):
        total = total + seen_ref[d] + other_ref[d]
    mean = jnp.sum(total, axis=0, keepdims=True) / SAMPLE_TOTAL

    me = me_ref[0]

    def at(turn, other):
        place = (me + 2 * (turns - turn)) & (2 * turns - 1)
        place = place ^ 1 if other else place
        return pl.ds(pl.multiple_of(place * share, share), share)

    for d in range(turns):
        state_ref[at(d, False), :] = seen_ref[d] - mean
        state_ref[at(d, True), :] = other_ref[d] - mean
    state_ref[SAMPLE_TOTAL:, :] = jnp.broadcast_to(value - mean, (8, n))
    anomaly = state_ref[0:SAMPLE_TOTAL, :]
    minus_ref[...] = anomaly
    eye = lax.broadcasted_iota(jnp.int32, (NOBS, NOBS), 0) == lax.broadcasted_iota(jnp.int32, (NOBS, NOBS), 1)
    for j in range(blocks):
        low, high = NOBS * j, NOBS * (j + 1)
        cov = dot6(anomaly[:, low:], anomaly[:, low:high], TN) / (SAMPLE_TOTAL - 1)
        cov_ref[low:high, low:high] = cov[:NOBS] + jnp.where(eye, var[:, low:high], 0.0)
        if high < n:
            cov_ref[high:, low:high] = cov[NOBS:]
    for j in range(blocks):
        low, high = NOBS * j, NOBS * (j + 1)
        if j == blocks - 1:
            mean_step = gain_ref[SAMPLE_TOTAL : SAMPLE_TOTAL + 1, :low]
            left = (mean_step - minus_ref[:, :low]) * (1.0 / (SAMPLE_TOTAL - 1))
            total_ref[...] = dot3(left, gain_ref[0:SAMPLE_TOTAL, :low], NT)
        root = jnp.sqrt(jnp.broadcast_to(var[:, low:high], (NOBS, NOBS))).T
        inv_low, inv_sum = factor(cov_ref[low:high, low:high], root)
        rest = high < n
        if rest:
            below = dot6(cov_ref[high:, low:high], inv_low, NT)
            for at in range(high, n, NOBS):
                change = dot6(below[at - high :], below[at - high : at - high + NOBS], NT)
                cov_ref[at:, at : at + NOBS] = cov_ref[at:, at : at + NOBS] - change
            below = halves(below)
        inv_low, inv_sum = halves(inv_low), halves(inv_sum)
        gain = dot_split(halves(state_ref[:, low:high]), inv_low, NT)
        minus = dot_split(halves(minus_ref[:, low:high]), inv_sum, NT)
        gain_ref[:, low:high] = gain
        if rest:
            state_ref[:, high:] = state_ref[:, high:] - dot_split(halves(gain), below, NT)
            minus_ref[:, high:] = minus_ref[:, high:] - dot_split(halves(minus), below, NT)
        minus_ref[:, low:high] = minus
    low = n - NOBS
    left = (gain_ref[SAMPLE_TOTAL : SAMPLE_TOTAL + 1, low:] - minus_ref[:, low:]) * (1.0 / (SAMPLE_TOTAL - 1))
    out_ref[...] = total_ref[...] + dot3(left, gain_ref[0:SAMPLE_TOTAL, low:], NT)


def update_kernel(transform_ref, cells_ref, out_ref):
    transform = halves(transform_ref[...])
    for r in range(0, 8, 2):
        at = [pl.ds(r + i, SAMPLE_TOTAL, stride=8) for i in range(2)]
        field = jnp.concatenate([cells_ref[a, :] for a in at], axis=1)
        new = field + dot_split(transform, halves(field), NN)
        for i in range(2):
            out_ref[at[i], :] = new[:, 128 * i : 128 * i + 128]


def stack_kernel(*refs):
    for i, ref in enumerate(refs[:-1]):
        refs[-1][i] = ref[...]


def join_kernel(parts_ref, out_ref, arrived):
    copies = []
    for h in range(2):
        for q in range(4):
            place = out_ref.at[:, 8 * h : 8 * h + 8, 128 * q : 128 * q + 128]
            copies.append(pltpu.make_async_copy(parts_ref.at[4 * h + q], place, arrived.at[4 * h + q]))
    for copy in copies:
        copy.start()
    for copy in copies:
        copy.wait()


def call(kernel, out_shape, scratch=(), grid=(), scalars=0, in_specs=None, out_specs=None, flops=0, bytes_accessed=0, limit=MEDIUM):
    specs = {} if in_specs is None else {"in_specs": in_specs, "out_specs": out_specs}
    return pl.pallas_call(
        kernel,
        out_shape=out_shape,
        grid_spec=pltpu.PrefetchScalarGridSpec(
            num_scalar_prefetch=scalars, grid=grid, scratch_shapes=list(scratch), **specs
        ),
        compiler_params=pltpu.CompilerParams(vmem_limit_bytes=limit),
        cost_estimate=pl.CostEstimate(flops=flops, bytes_accessed=bytes_accessed, transcendentals=0),
    )


def spec(shape, *axes):
    places = tuple(axes) + (None,) * (len(shape) - len(axes))
    return pl.BlockSpec(shape, lambda i, *scalars: tuple(0 if p is None else i for p in places))


def body(prior_samples, neighbour_weights, obs_cell, obs_value, obs_var, block_order):
    f32 = jnp.float32
    members, rows, width = prior_samples.shape
    mem_count, cell_count = lax.axis_size("mem"), lax.axis_size("cell")
    me = lax.axis_index("mem")
    base = (lax.axis_index("cell") * rows).reshape(1)
    shape = jax.ShapeDtypeStruct
    steps = 2
    step = members // steps
    side = 4
    forward = [(i, i + 1) for i in range(cell_count - 1)]
    backward = [(i + 1, i) for i in range(cell_count - 1)]
    swap = [(i, i ^ 1) for i in range(mem_count)]

    def along_x(value, d):
        return lax.ppermute(value, "mem", [(i, (i + 2 * d) % mem_count) for i in range(mem_count)])

    def ring(value, phase, d):
        def target(m, i):
            z, y = i % side, i // side
            if (m + phase) % 2 == 0:
                z = (z + d) % side
            else:
                y = (y + d) % side
            return m * cell_count + y * side + z

        places = [(m, i) for m in range(mem_count) for i in range(cell_count)]
        return lax.ppermute(value, ("mem", "cell"), [(m * cell_count + i, target(m, i)) for m, i in places])

    low = lax.ppermute(prior_samples[:, rows - 1, :], "cell", forward)
    high = lax.ppermute(prior_samples[:, 0, :], "cell", backward)
    smem = pl.BlockSpec(memory_space=pltpu.SMEM)
    seen_shape = shape((members, ALL_OBS), f32)
    pieces, seen = call(
        forecast_kernel,
        (shape((mem_count, members, 8, 128), f32), seen_shape),
        [
            pltpu.VMEM((width, ALL_OBS), jnp.bfloat16),
            pltpu.VMEM((step * rows, width), f32),
        ],
        grid=(steps,),
        in_specs=[
            smem,
            smem,
            spec((step, rows, width), 0),
            spec((4, rows, width)),
            spec(obs_cell.shape),
        ],
        out_specs=[spec((mem_count, step, 8, 128), None, 0), spec((step, ALL_OBS), 0)],
        flops=2_000_000_000,
        bytes_accessed=4_000_000,
        limit=LARGE,
    )(block_order, base, prior_samples, neighbour_weights, obs_cell)
    seen = call(
        halo_kernel,
        seen_shape,
        grid=(1,),
        in_specs=[
            smem,
            smem,
            spec((members, ALL_OBS)),
            spec((members, width)),
            spec((members, width)),
            spec((4, rows, width)),
            spec(obs_cell.shape),
        ],
        out_specs=spec((members, ALL_OBS)),
        limit=SMALL,
    )(block_order, base, seen, low, high, neighbour_weights, obs_cell)

    tiles = spec((4 * members * 8, 128), 0)
    pieces = pl.pallas_call(
        edge_kernel,
        out_shape=shape((mem_count * members * 8, 128), f32),
        grid=(2,),
        in_specs=[tiles, spec((4, rows, width)), spec((members, width)), spec((members, width))],
        out_specs=tiles,
        input_output_aliases={0: 0},
        compiler_params=pltpu.CompilerParams(vmem_limit_bytes=MEDIUM),
    )(pieces.reshape(mem_count * members * 8, 128), neighbour_weights, low, high)
    pieces = pieces.reshape(mem_count, members, 8, 128)

    for phase in range(2):
        others = [ring(seen, phase, d) for d in (1, 3, 2)]
        if phase == 0:
            pieces, *others = lax.optimization_barrier([pieces] + others)
        seen = call(sum_kernel, seen_shape, limit=SMALL)(seen, *others)
    one, three, two = along_x(seen, 1), along_x(seen, 3), along_x(seen, 2)
    one, two, three, pieces = lax.optimization_barrier((one, two, three, pieces))
    cells = lax.all_to_all(pieces, "mem", 0, 0)
    seen = call(stack_kernel, shape((4, members, ALL_OBS), f32), limit=SMALL)(seen, one, two, three)
    other = lax.ppermute(seen, "mem", swap)

    square = (ALL_OBS, ALL_OBS)
    transform = call(
        transform_kernel,
        shape(square, f32),
        [
            pltpu.VMEM(square, f32),
            pltpu.VMEM((SAMPLE_TOTAL + 8, ALL_OBS), f32),
            pltpu.VMEM((SAMPLE_TOTAL + 8, ALL_OBS), f32),
            pltpu.VMEM(square, f32),
            pltpu.VMEM(square, f32),
        ],
        grid=(1,),
        scalars=2,
        in_specs=[
            spec((4, members, ALL_OBS)),
            spec((4, members, ALL_OBS)),
            spec(obs_value.shape),
            spec(obs_var.shape),
        ],
        out_specs=spec(square),
        flops=20_000_000_000,
        bytes_accessed=2_000_000,
    )(block_order, me.reshape(1), seen, other, obs_value, obs_var)

    cells = cells.reshape(SAMPLE_TOTAL * 8, 128)
    new = call(update_kernel, shape(cells.shape, f32), flops=3_000_000_000, bytes_accessed=4_000_000)(
        transform, cells
    )
    new = lax.all_to_all(new.reshape(mem_count, members, 8, 128), "mem", 0, 0)
    anywhere = pl.BlockSpec(memory_space=pl.ANY)
    return call(
        join_kernel,
        shape(prior_samples.shape, f32),
        [pltpu.SemaphoreType.DMA((8,))],
        grid=(1,),
        in_specs=[anywhere],
        out_specs=anywhere,
        bytes_accessed=4_000_000,
        limit=SMALL,
    )(new)


def solution(mesh):
    return jax.shard_map(
        body,
        mesh=mesh,
        in_specs=(P("mem", "cell", None), P(None, "cell", None), P(), P(), P(), P()),
        out_specs=P("mem", "cell", None),
        check_vma=False,
    )
```

```python
import functools

import jax
import jax.numpy as jnp
from jax import lax
from jax.experimental import pallas as pl
from jax.experimental.pallas import tpu as pltpu
from jax.sharding import PartitionSpec as P

SAMPLE_TOTAL = 512
NOBS = 128
ALL_OBS = 512
HIGHEST = lax.Precision.HIGHEST
NT = (((1,), (1,)), ((), ()))
TN = (((0,), (0,)), ((), ()))
NN = (((1,), (0,)), ((), ()))
LARGE = 60 * 1024 * 1024
MEDIUM = 20 * 1024 * 1024
SMALL = 8 * 1024 * 1024


def halves(value):
    high = value.astype(jnp.bfloat16)
    low = (value - high.astype(jnp.float32)).astype(jnp.bfloat16)
    return high, low


def dot_split(left, right, dims):
    f32 = jnp.float32
    left_high, left_low = left
    right_high, right_low = right
    small = lax.dot_general(left_low, right_high, dims, preferred_element_type=f32)
    small = small + lax.dot_general(left_high, right_low, dims, preferred_element_type=f32)
    return small + lax.dot_general(left_high, right_high, dims, preferred_element_type=f32)


def dot3(left, right, dims):
    return dot_split(halves(left), halves(right), dims)


def dot6(left, right, dims):
    return lax.dot_general(
        left, right, dims, precision=HIGHEST, preferred_element_type=jnp.float32
    )


def forecast_kernel(order_ref, base_ref, x_ref, weight_ref, cell_ref, piece_ref, own_ref, pick_ref, flat_ref):
    members, rows, width = x_ref.shape
    col_at = lax.broadcasted_iota(jnp.int32, (rows, width), 1)
    row_at = lax.broadcasted_iota(jnp.int32, (rows, width), 0)
    east, west, north, south = [weight_ref[i] for i in range(4)]
    cell = jnp.concatenate([cell_ref[pl.ds(order_ref[j], 1), :] for j in range(order_ref.shape[0])], axis=1)
    at_row = (cell >> 9) - base_ref[0]

    @pl.when(pl.program_id(0) == 0)
    def _():
        at_col = cell & (width - 1)
        pick = lax.broadcasted_iota(jnp.int32, (width, ALL_OBS), 0) == at_col
        pick_ref[...] = pick.astype(jnp.bfloat16)

    def member(m, carry):
        x = x_ref[m]
        to_east = jnp.where(col_at == width - 1, 0.0, pltpu.roll(x, width - 1, 1))
        to_west = jnp.where(col_at == 0, 0.0, pltpu.roll(x, 1, 1))
        to_north = jnp.where(row_at == 0, 0.0, pltpu.roll(x, 1, 0))
        to_south = jnp.where(row_at == rows - 1, 0.0, pltpu.roll(x, rows - 1, 0))
        f = (
            x
            + east * (to_east - x)
            + west * (to_west - x)
            + north * (to_north - x)
            + south * (to_south - x)
        )
        flat_ref[pl.ds(pl.multiple_of(m * rows, rows), rows), :] = f
        for h in range(2):
            for q in range(4):
                piece_ref[4 * h + q, m] = f[8 * h : 8 * h + 8, 128 * q : 128 * q + 128]
        return carry

    lax.fori_loop(0, members, member, 0, unroll=8)
    own_row = (lax.broadcasted_iota(jnp.int32, (rows, ALL_OBS), 0) == at_row).astype(jnp.float32)
    pick = pick_ref[...]
    part = 8
    for g in range(members // part):
        value = flat_ref[g * part * rows : (g + 1) * part * rows, :]
        total = picked(value, pick).reshape(part, rows, ALL_OBS) * own_row[None]
        own_ref[part * g : part * g + part, :] = jnp.sum(total, axis=1)


def picked(value, pick):
    total = None
    for _ in range(3):
        cut = value.astype(jnp.bfloat16)
        value = value - cut.astype(jnp.float32)
        term = lax.dot_general(cut, pick, NN, preferred_element_type=jnp.float32)
        total = term if total is None else total + term
    return total


def halo_kernel(order_ref, base_ref, own_ref, low_ref, high_ref, weight_ref, cell_ref, out_ref):
    members, width = low_ref.shape
    rows = weight_ref.shape[1]
    cell = jnp.concatenate([cell_ref[pl.ds(order_ref[j], 1), :] for j in range(order_ref.shape[0])], axis=1)
    at_row = (cell >> 9) - base_ref[0]
    pick = lax.broadcasted_iota(jnp.int32, (width, ALL_OBS), 0) == (cell & (width - 1))
    edges = [low_ref[...], high_ref[...], weight_ref[2, 0:8, :], weight_ref[3, rows - 8 :, :]]
    edges = picked(jnp.concatenate(edges, axis=0), pick.astype(jnp.bfloat16))
    first = edges[2 * members : 2 * members + 1] * edges[0:members]
    last = edges[2 * members + 15 : 2 * members + 16] * edges[members : 2 * members]
    out_ref[...] = own_ref[...] + jnp.where(at_row == 0, first, 0.0) + jnp.where(at_row == rows - 1, last, 0.0)


def edge_kernel(piece_ref, weight_ref, low_ref, high_ref, out_ref):
    members = low_ref.shape[0]
    rows = weight_ref.shape[1]
    upper = pl.program_id(0) == 0
    out_ref[...] = piece_ref[...]
    weight = jnp.where(upper, weight_ref[2, 0:1, :], weight_ref[3, rows - 1 : rows, :])
    change = weight * jnp.where(upper, low_ref[...], high_ref[...])

    def add(first):
        for q in range(4):
            at = pl.ds(members * 8 * q + first, members, stride=8)
            out_ref[at, :] = out_ref[at, :] + change[:, 128 * q : 128 * q + 128]

    pl.when(upper)(lambda: add(0))
    pl.when(jnp.logical_not(upper))(lambda: add(7))


def sum_kernel(*refs):
    total = refs[0][...]
    for ref in refs[1:-1]:
        total = total + ref[...]
    refs[-1][...] = total


def over_rows(value, row):
    return jnp.broadcast_to(value[row : row + 1, :], (8, NOBS))


def over_lanes(value, lane):
    return jnp.broadcast_to(value[:, lane : lane + 1], (8, NOBS))


def factor(block, root):
    count = NOBS // 8
    sub = lax.broadcasted_iota(jnp.int32, (8, NOBS), 0)
    lane = lax.broadcasted_iota(jnp.int32, (8, NOBS), 1)
    rows = [block[8 * i : 8 * i + 8, :] for i in range(count)]
    shifted = [(lane == sub + 8 * i).astype(jnp.float32) for i in range(count)]
    inverse = [None] * count
    for b in range(count):
        panel = rows[b]
        column = [over_lanes(panel, 8 * b + k) for k in range(8)]
        done = jnp.zeros((8, NOBS), jnp.float32)
        plus = shifted[b]
        inv_roots = []
        for k in range(8):
            at = 8 * b + k
            pivot = over_rows(column[k], k)
            inv_root = lax.rsqrt(pivot)
            inv = pl.reciprocal(pivot)
            inv_roots.append(inv_root)
            row = jnp.where(lane == at, 1.0, over_rows(panel, k))
            done = jnp.where(sub == k, row * inv_root, done)
            away = jnp.where(sub == k, -1.0, column[k])
            panel = jnp.where((sub == k) | (lane == at), 0.0, panel) - (away * row) * inv
            plus_row = over_rows(plus, k) / (pivot * inv_root + over_rows(root[8 * b : 8 * b + 8, :], k))
            below = jnp.where(sub > k, column[k] * inv_root, 0.0)
            plus = jnp.where(sub == k, plus_row, plus - below * plus_row)
            for j in range(k + 1, 8):
                step = away * over_rows(column[j], k)
                column[j] = jnp.where(sub == k, 0.0, column[j]) - step * inv
        inverse[b] = jnp.where(lane <= sub + 8 * b, done, 0.0)
        shifted[b] = plus
        if b == count - 1:
            break
        for k in reversed(range(8)):
            above = jnp.where(sub < k, over_lanes(done, 8 * b + k), 0.0)
            row = over_rows(plus, k) * inv_roots[k]
            plus = jnp.where(sub == k, row, plus - above * row)
        panel_rows = [over_rows(panel, k) for k in range(8)]
        plus_rows = [over_rows(plus, k) for k in range(8)]
        inside = (lane >= 8 * b) & (lane < 8 * b + 8)
        for r in range(b + 1, count):
            left = [over_lanes(rows[r], 8 * b + k) for k in range(8)]
            new = jnp.where(inside, 0.0, rows[r])
            new_shifted = shifted[r]
            for k in range(8):
                new = new - left[k] * panel_rows[k]
                new_shifted = new_shifted - left[k] * plus_rows[k]
            rows[r] = new
            shifted[r] = new_shifted
    return jnp.concatenate(inverse, axis=0), jnp.concatenate(shifted, axis=0)


def transform_kernel(
    block_ref, me_ref, seen_ref, other_ref, value_ref, var_ref,
    out_ref, cov_ref, state_ref, gain_ref, minus_ref, total_ref,
):
    n = ALL_OBS
    blocks = n // NOBS
    turns, share = seen_ref.shape[0], seen_ref.shape[1]
    value = jnp.concatenate([value_ref[pl.ds(block_ref[j], 1), :] for j in range(blocks)], axis=1)
    var = jnp.concatenate([var_ref[pl.ds(block_ref[j], 1), :] for j in range(blocks)], axis=1)
    total = seen_ref[0] + other_ref[0]
    for d in range(1, turns):
        total = total + seen_ref[d] + other_ref[d]
    mean = jnp.sum(total, axis=0, keepdims=True) / SAMPLE_TOTAL

    me = me_ref[0]

    def at(turn, other):
        place = (me + 2 * (turns - turn)) & (2 * turns - 1)
        place = place ^ 1 if other else place
        return pl.ds(pl.multiple_of(place * share, share), share)

    for d in range(turns):
        state_ref[at(d, False), :] = seen_ref[d] - mean
        state_ref[at(d, True), :] = other_ref[d] - mean
    state_ref[SAMPLE_TOTAL:, :] = jnp.broadcast_to(value - mean, (8, n))
    anomaly = state_ref[0:SAMPLE_TOTAL, :]
    minus_ref[...] = anomaly
    eye = lax.broadcasted_iota(jnp.int32, (NOBS, NOBS), 0) == lax.broadcasted_iota(jnp.int32, (NOBS, NOBS), 1)
    for j in range(blocks):
        low, high = NOBS * j, NOBS * (j + 1)
        cov = dot6(anomaly[:, low:], anomaly[:, low:high], TN) / (SAMPLE_TOTAL - 1)
        cov_ref[low:high, low:high] = cov[:NOBS] + jnp.where(eye, var[:, low:high], 0.0)
        if high < n:
            cov_ref[high:, low:high] = cov[NOBS:]
    for j in range(blocks):
        low, high = NOBS * j, NOBS * (j + 1)
        if j == blocks - 1:
            mean_step = gain_ref[SAMPLE_TOTAL : SAMPLE_TOTAL + 1, :low]
            left = (mean_step - minus_ref[:, :low]) * (1.0 / (SAMPLE_TOTAL - 1))
            total_ref[...] = dot3(left, gain_ref[0:SAMPLE_TOTAL, :low], NT)
        root = jnp.sqrt(jnp.broadcast_to(var[:, low:high], (NOBS, NOBS))).T
        inv_low, inv_sum = factor(cov_ref[low:high, low:high], root)
        rest = high < n
        if rest:
            below = dot6(cov_ref[high:, low:high], inv_low, NT)
            for at in range(high, n, NOBS):
                change = dot6(below[at - high :], below[at - high : at - high + NOBS], NT)
                cov_ref[at:, at : at + NOBS] = cov_ref[at:, at : at + NOBS] - change
        gain = dot6(state_ref[:, low:high], inv_low, NT)
        minus = dot6(minus_ref[:, low:high], inv_sum, NT)
        gain_ref[:, low:high] = gain
        if rest:
            state_ref[:, high:] = state_ref[:, high:] - dot6(gain, below, NT)
            minus_ref[:, high:] = minus_ref[:, high:] - dot6(minus, below, NT)
        minus_ref[:, low:high] = minus
    low = n - NOBS
    left = (gain_ref[SAMPLE_TOTAL : SAMPLE_TOTAL + 1, low:] - minus_ref[:, low:]) * (1.0 / (SAMPLE_TOTAL - 1))
    out_ref[...] = total_ref[...] + dot3(left, gain_ref[0:SAMPLE_TOTAL, low:], NT)


def update_kernel(transform_ref, cells_ref, out_ref):
    transform = halves(transform_ref[...])
    for r in range(0, 8, 2):
        at = [pl.ds(r + i, SAMPLE_TOTAL, stride=8) for i in range(2)]
        field = jnp.concatenate([cells_ref[a, :] for a in at], axis=1)
        mean = jnp.sum(field, axis=0, keepdims=True) / SAMPLE_TOTAL
        new = field + dot_split(transform, halves(field - mean), NN)
        for i in range(2):
            out_ref[at[i], :] = new[:, 128 * i : 128 * i + 128]


def stack_kernel(*refs):
    for i, ref in enumerate(refs[:-1]):
        refs[-1][i] = ref[...]


def join_kernel(parts_ref, out_ref, arrived):
    copies = []
    for h in range(2):
        for q in range(4):
            place = out_ref.at[:, 8 * h : 8 * h + 8, 128 * q : 128 * q + 128]
            copies.append(pltpu.make_async_copy(parts_ref.at[4 * h + q], place, arrived.at[4 * h + q]))
    for copy in copies:
        copy.start()
    for copy in copies:
        copy.wait()


def call(kernel, out_shape, scratch=(), grid=(), scalars=0, in_specs=None, out_specs=None, flops=0, bytes_accessed=0, limit=MEDIUM):
    specs = {} if in_specs is None else {"in_specs": in_specs, "out_specs": out_specs}
    return pl.pallas_call(
        kernel,
        out_shape=out_shape,
        grid_spec=pltpu.PrefetchScalarGridSpec(
            num_scalar_prefetch=scalars, grid=grid, scratch_shapes=list(scratch), **specs
        ),
        compiler_params=pltpu.CompilerParams(vmem_limit_bytes=limit),
        cost_estimate=pl.CostEstimate(flops=flops, bytes_accessed=bytes_accessed, transcendentals=0),
    )


def spec(shape, *axes):
    places = tuple(axes) + (None,) * (len(shape) - len(axes))
    return pl.BlockSpec(shape, lambda i, *scalars: tuple(0 if p is None else i for p in places))


def body(prior_samples, neighbour_weights, obs_cell, obs_value, obs_var, block_order):
    f32 = jnp.float32
    members, rows, width = prior_samples.shape
    mem_count, cell_count = lax.axis_size("mem"), lax.axis_size("cell")
    me = lax.axis_index("mem")
    base = (lax.axis_index("cell") * rows).reshape(1)
    shape = jax.ShapeDtypeStruct
    steps = 2
    step = members // steps
    side = 4
    forward = [(i, i + 1) for i in range(cell_count - 1)]
    backward = [(i + 1, i) for i in range(cell_count - 1)]
    swap = [(i, i ^ 1) for i in range(mem_count)]

    def along_x(value, d):
        return lax.ppermute(value, "mem", [(i, (i + 2 * d) % mem_count) for i in range(mem_count)])

    def ring(value, phase, d):
        def target(m, i):
            z, y = i % side, i // side
            if (m + phase) % 2 == 0:
                z = (z + d) % side
            else:
                y = (y + d) % side
            return m * cell_count + y * side + z

        places = [(m, i) for m in range(mem_count) for i in range(cell_count)]
        return lax.ppermute(value, ("mem", "cell"), [(m * cell_count + i, target(m, i)) for m, i in places])

    low = lax.ppermute(prior_samples[:, rows - 1, :], "cell", forward)
    high = lax.ppermute(prior_samples[:, 0, :], "cell", backward)
    smem = pl.BlockSpec(memory_space=pltpu.SMEM)
    seen_shape = shape((members, ALL_OBS), f32)
    pieces, seen = call(
        forecast_kernel,
        (shape((mem_count, members, 8, 128), f32), seen_shape),
        [
            pltpu.VMEM((width, ALL_OBS), jnp.bfloat16),
            pltpu.VMEM((step * rows, width), f32),
        ],
        grid=(steps,),
        in_specs=[
            smem,
            smem,
            spec((step, rows, width), 0),
            spec((4, rows, width)),
            spec(obs_cell.shape),
        ],
        out_specs=[spec((mem_count, step, 8, 128), None, 0), spec((step, ALL_OBS), 0)],
        flops=2_000_000_000,
        bytes_accessed=4_000_000,
        limit=LARGE,
    )(block_order, base, prior_samples, neighbour_weights, obs_cell)
    seen = call(
        halo_kernel,
        seen_shape,
        grid=(1,),
        in_specs=[
            smem,
            smem,
            spec((members, ALL_OBS)),
            spec((members, width)),
            spec((members, width)),
            spec((4, rows, width)),
            spec(obs_cell.shape),
        ],
        out_specs=spec((members, ALL_OBS)),
        limit=SMALL,
    )(block_order, base, seen, low, high, neighbour_weights, obs_cell)

    tiles = spec((4 * members * 8, 128), 0)
    pieces = pl.pallas_call(
        edge_kernel,
        out_shape=shape((mem_count * members * 8, 128), f32),
        grid=(2,),
        in_specs=[tiles, spec((4, rows, width)), spec((members, width)), spec((members, width))],
        out_specs=tiles,
        input_output_aliases={0: 0},
        compiler_params=pltpu.CompilerParams(vmem_limit_bytes=MEDIUM),
    )(pieces.reshape(mem_count * members * 8, 128), neighbour_weights, low, high)
    pieces = pieces.reshape(mem_count, members, 8, 128)

    for phase in range(2):
        others = [ring(seen, phase, d) for d in (1, 3, 2)]
        if phase == 0:
            pieces, *others = lax.optimization_barrier([pieces] + others)
        seen = call(sum_kernel, seen_shape, limit=SMALL)(seen, *others)
    one, three, two = along_x(seen, 1), along_x(seen, 3), along_x(seen, 2)
    one, two, three, pieces = lax.optimization_barrier((one, two, three, pieces))
    cells = lax.all_to_all(pieces, "mem", 0, 0)
    seen = call(stack_kernel, shape((4, members, ALL_OBS), f32), limit=SMALL)(seen, one, two, three)
    other = lax.ppermute(seen, "mem", swap)

    square = (ALL_OBS, ALL_OBS)
    transform = call(
        transform_kernel,
        shape(square, f32),
        [
            pltpu.VMEM(square, f32),
            pltpu.VMEM((SAMPLE_TOTAL + 8, ALL_OBS), f32),
            pltpu.VMEM((SAMPLE_TOTAL + 8, ALL_OBS), f32),
            pltpu.VMEM(square, f32),
            pltpu.VMEM(square, f32),
        ],
        grid=(1,),
        scalars=2,
        in_specs=[
            spec((4, members, ALL_OBS)),
            spec((4, members, ALL_OBS)),
            spec(obs_value.shape),
            spec(obs_var.shape),
        ],
        out_specs=spec(square),
        flops=20_000_000_000,
        bytes_accessed=2_000_000,
    )(block_order, me.reshape(1), seen, other, obs_value, obs_var)

    cells = cells.reshape(SAMPLE_TOTAL * 8, 128)
    new = call(update_kernel, shape(cells.shape, f32), flops=3_000_000_000, bytes_accessed=4_000_000)(
        transform, cells
    )
    new = lax.all_to_all(new.reshape(mem_count, members, 8, 128), "mem", 0, 0)
    anywhere = pl.BlockSpec(memory_space=pl.ANY)
    return call(
        join_kernel,
        shape(prior_samples.shape, f32),
        [pltpu.SemaphoreType.DMA((8,))],
        grid=(1,),
        in_specs=[anywhere],
        out_specs=anywhere,
        bytes_accessed=4_000_000,
        limit=SMALL,
    )(new)


def solution(mesh):
    return jax.shard_map(
        body,
        mesh=mesh,
        in_specs=(P("mem", "cell", None), P(None, "cell", None), P(), P(), P(), P()),
        out_specs=P("mem", "cell", None),
        check_vma=False,
    )
```

```python
import functools

import jax
import jax.numpy as jnp
from jax import lax
from jax.experimental import pallas as pl
from jax.experimental.pallas import tpu as pltpu
from jax.sharding import PartitionSpec as P

SAMPLE_TOTAL = 512
NOBS = 128
ALL_OBS = 512
HIGHEST = lax.Precision.HIGHEST
NT = (((1,), (1,)), ((), ()))
TN = (((0,), (0,)), ((), ()))
NN = (((1,), (0,)), ((), ()))
LARGE = 60 * 1024 * 1024
MEDIUM = 20 * 1024 * 1024
SMALL = 8 * 1024 * 1024


def halves(value):
    high = value.astype(jnp.bfloat16)
    low = (value - high.astype(jnp.float32)).astype(jnp.bfloat16)
    return high, low


def dot_split(left, right, dims):
    f32 = jnp.float32
    left_high, left_low = left
    right_high, right_low = right
    small = lax.dot_general(left_low, right_high, dims, preferred_element_type=f32)
    small = small + lax.dot_general(left_high, right_low, dims, preferred_element_type=f32)
    return small + lax.dot_general(left_high, right_high, dims, preferred_element_type=f32)


def dot3(left, right, dims):
    return dot_split(halves(left), halves(right), dims)


def dot6(left, right, dims):
    return lax.dot_general(
        left, right, dims, precision=HIGHEST, preferred_element_type=jnp.float32
    )


def forecast_kernel(order_ref, base_ref, x_ref, weight_ref, cell_ref, piece_ref, own_ref, pick_ref, flat_ref):
    members, rows, width = x_ref.shape
    col_at = lax.broadcasted_iota(jnp.int32, (rows, width), 1)
    row_at = lax.broadcasted_iota(jnp.int32, (rows, width), 0)
    east, west, north, south = [weight_ref[i] for i in range(4)]
    cell = jnp.concatenate([cell_ref[pl.ds(order_ref[j], 1), :] for j in range(order_ref.shape[0])], axis=1)
    at_row = (cell >> 9) - base_ref[0]

    @pl.when(pl.program_id(0) == 0)
    def _():
        at_col = cell & (width - 1)
        pick = lax.broadcasted_iota(jnp.int32, (width, ALL_OBS), 0) == at_col
        pick_ref[...] = pick.astype(jnp.bfloat16)

    def member(m, carry):
        x = x_ref[m]
        to_east = jnp.where(col_at == width - 1, 0.0, pltpu.roll(x, width - 1, 1))
        to_west = jnp.where(col_at == 0, 0.0, pltpu.roll(x, 1, 1))
        to_north = jnp.where(row_at == 0, 0.0, pltpu.roll(x, 1, 0))
        to_south = jnp.where(row_at == rows - 1, 0.0, pltpu.roll(x, rows - 1, 0))
        f = (
            x
            + east * (to_east - x)
            + west * (to_west - x)
            + north * (to_north - x)
            + south * (to_south - x)
        )
        flat_ref[pl.ds(pl.multiple_of(m * rows, rows), rows), :] = f
        for h in range(2):
            for q in range(4):
                piece_ref[4 * h + q, m] = f[8 * h : 8 * h + 8, 128 * q : 128 * q + 128]
        return carry

    lax.fori_loop(0, members, member, 0, unroll=32)
    own_row = (lax.broadcasted_iota(jnp.int32, (rows, ALL_OBS), 0) == at_row).astype(jnp.float32)
    pick = pick_ref[...]
    part = 8
    for g in range(members // part):
        value = flat_ref[g * part * rows : (g + 1) * part * rows, :]
        total = picked(value, pick).reshape(part, rows, ALL_OBS) * own_row[None]
        own_ref[part * g : part * g + part, :] = jnp.sum(total, axis=1)


def picked(value, pick):
    total = None
    for _ in range(3):
        cut = value.astype(jnp.bfloat16)
        value = value - cut.astype(jnp.float32)
        term = lax.dot_general(cut, pick, NN, preferred_element_type=jnp.float32)
        total = term if total is None else total + term
    return total


def halo_kernel(order_ref, base_ref, own_ref, low_ref, high_ref, weight_ref, cell_ref, out_ref):
    members, width = low_ref.shape
    rows = weight_ref.shape[1]
    cell = jnp.concatenate([cell_ref[pl.ds(order_ref[j], 1), :] for j in range(order_ref.shape[0])], axis=1)
    at_row = (cell >> 9) - base_ref[0]
    pick = lax.broadcasted_iota(jnp.int32, (width, ALL_OBS), 0) == (cell & (width - 1))
    edges = [low_ref[...], high_ref[...], weight_ref[2, 0:8, :], weight_ref[3, rows - 8 :, :]]
    edges = picked(jnp.concatenate(edges, axis=0), pick.astype(jnp.bfloat16))
    first = edges[2 * members : 2 * members + 1] * edges[0:members]
    last = edges[2 * members + 15 : 2 * members + 16] * edges[members : 2 * members]
    out_ref[...] = own_ref[...] + jnp.where(at_row == 0, first, 0.0) + jnp.where(at_row == rows - 1, last, 0.0)


def edge_kernel(piece_ref, weight_ref, low_ref, high_ref, out_ref):
    members = low_ref.shape[0]
    rows = weight_ref.shape[1]
    upper = pl.program_id(0) == 0
    out_ref[...] = piece_ref[...]
    weight = jnp.where(upper, weight_ref[2, 0:1, :], weight_ref[3, rows - 1 : rows, :])
    change = weight * jnp.where(upper, low_ref[...], high_ref[...])

    def add(first):
        for q in range(4):
            at = pl.ds(members * 8 * q + first, members, stride=8)
            out_ref[at, :] = out_ref[at, :] + change[:, 128 * q : 128 * q + 128]

    pl.when(upper)(lambda: add(0))
    pl.when(jnp.logical_not(upper))(lambda: add(7))


def sum_kernel(*refs):
    total = refs[0][...]
    for ref in refs[1:-1]:
        total = total + ref[...]
    refs[-1][...] = total


def over_rows(value, row):
    return jnp.broadcast_to(value[row : row + 1, :], (8, NOBS))


def over_lanes(value, lane):
    return jnp.broadcast_to(value[:, lane : lane + 1], (8, NOBS))


def factor(block, root):
    count = NOBS // 8
    sub = lax.broadcasted_iota(jnp.int32, (8, NOBS), 0)
    lane = lax.broadcasted_iota(jnp.int32, (8, NOBS), 1)
    rows = [block[8 * i : 8 * i + 8, :] for i in range(count)]
    shifted = [(lane == sub + 8 * i).astype(jnp.float32) for i in range(count)]
    inverse = [None] * count
    for b in range(count):
        panel = rows[b]
        column = [over_lanes(panel, 8 * b + k) for k in range(8)]
        done = jnp.zeros((8, NOBS), jnp.float32)
        plus = shifted[b]
        inv_roots = []
        for k in range(8):
            at = 8 * b + k
            pivot = over_rows(column[k], k)
            inv_root = lax.rsqrt(pivot)
            inv = pl.reciprocal(pivot)
            inv_roots.append(inv_root)
            row = jnp.where(lane == at, 1.0, over_rows(panel, k))
            done = jnp.where(sub == k, row * inv_root, done)
            away = jnp.where(sub == k, -1.0, column[k])
            panel = jnp.where((sub == k) | (lane == at), 0.0, panel) - (away * row) * inv
            plus_row = over_rows(plus, k) / (pivot * inv_root + over_rows(root[8 * b : 8 * b + 8, :], k))
            below = jnp.where(sub > k, column[k] * inv_root, 0.0)
            plus = jnp.where(sub == k, plus_row, plus - below * plus_row)
            for j in range(k + 1, 8):
                step = away * over_rows(column[j], k)
                column[j] = jnp.where(sub == k, 0.0, column[j]) - step * inv
        inverse[b] = jnp.where(lane <= sub + 8 * b, done, 0.0)
        shifted[b] = plus
        if b == count - 1:
            break
        for k in reversed(range(8)):
            above = jnp.where(sub < k, over_lanes(done, 8 * b + k), 0.0)
            row = over_rows(plus, k) * inv_roots[k]
            plus = jnp.where(sub == k, row, plus - above * row)
        panel_rows = [over_rows(panel, k) for k in range(8)]
        plus_rows = [over_rows(plus, k) for k in range(8)]
        inside = (lane >= 8 * b) & (lane < 8 * b + 8)
        for r in range(b + 1, count):
            left = [over_lanes(rows[r], 8 * b + k) for k in range(8)]
            new = jnp.where(inside, 0.0, rows[r])
            new_shifted = shifted[r]
            for k in range(8):
                new = new - left[k] * panel_rows[k]
                new_shifted = new_shifted - left[k] * plus_rows[k]
            rows[r] = new
            shifted[r] = new_shifted
    return jnp.concatenate(inverse, axis=0), jnp.concatenate(shifted, axis=0)


def transform_kernel(
    block_ref, me_ref, seen_ref, other_ref, value_ref, var_ref,
    out_ref, cov_ref, state_ref, gain_ref, minus_ref, total_ref,
):
    n = ALL_OBS
    blocks = n // NOBS
    turns, share = seen_ref.shape[0], seen_ref.shape[1]
    value = jnp.concatenate([value_ref[pl.ds(block_ref[j], 1), :] for j in range(blocks)], axis=1)
    var = jnp.concatenate([var_ref[pl.ds(block_ref[j], 1), :] for j in range(blocks)], axis=1)
    total = seen_ref[0] + other_ref[0]
    for d in range(1, turns):
        total = total + seen_ref[d] + other_ref[d]
    mean = jnp.sum(total, axis=0, keepdims=True) / SAMPLE_TOTAL

    me = me_ref[0]

    def at(turn, other):
        place = (me + 2 * (turns - turn)) & (2 * turns - 1)
        place = place ^ 1 if other else place
        return pl.ds(pl.multiple_of(place * share, share), share)

    for d in range(turns):
        state_ref[at(d, False), :] = seen_ref[d] - mean
        state_ref[at(d, True), :] = other_ref[d] - mean
    state_ref[SAMPLE_TOTAL:, :] = jnp.broadcast_to(value - mean, (8, n))
    anomaly = state_ref[0:SAMPLE_TOTAL, :]
    minus_ref[...] = anomaly
    eye = lax.broadcasted_iota(jnp.int32, (NOBS, NOBS), 0) == lax.broadcasted_iota(jnp.int32, (NOBS, NOBS), 1)
    for j in range(blocks):
        low, high = NOBS * j, NOBS * (j + 1)
        cov = dot6(anomaly[:, low:], anomaly[:, low:high], TN) / (SAMPLE_TOTAL - 1)
        cov_ref[low:high, low:high] = cov[:NOBS] + jnp.where(eye, var[:, low:high], 0.0)
        if high < n:
            cov_ref[high:, low:high] = cov[NOBS:]
    for j in range(blocks):
        low, high = NOBS * j, NOBS * (j + 1)
        if j == blocks - 1:
            mean_step = gain_ref[SAMPLE_TOTAL : SAMPLE_TOTAL + 1, :low]
            left = (mean_step - minus_ref[:, :low]) * (1.0 / (SAMPLE_TOTAL - 1))
            total_ref[...] = dot3(left, gain_ref[0:SAMPLE_TOTAL, :low], NT)
        root = jnp.sqrt(jnp.broadcast_to(var[:, low:high], (NOBS, NOBS))).T
        inv_low, inv_sum = factor(cov_ref[low:high, low:high], root)
        rest = high < n
        if rest:
            below = dot6(cov_ref[high:, low:high], inv_low, NT)
            for at in range(high, n, NOBS):
                change = dot6(below[at - high :], below[at - high : at - high + NOBS], NT)
                cov_ref[at:, at : at + NOBS] = cov_ref[at:, at : at + NOBS] - change
        gain = dot6(state_ref[:, low:high], inv_low, NT)
        minus = dot6(minus_ref[:, low:high], inv_sum, NT)
        gain_ref[:, low:high] = gain
        if rest:
            state_ref[:, high:] = state_ref[:, high:] - dot6(gain, below, NT)
            minus_ref[:, high:] = minus_ref[:, high:] - dot6(minus, below, NT)
        minus_ref[:, low:high] = minus
    low = n - NOBS
    left = (gain_ref[SAMPLE_TOTAL : SAMPLE_TOTAL + 1, low:] - minus_ref[:, low:]) * (1.0 / (SAMPLE_TOTAL - 1))
    out_ref[...] = total_ref[...] + dot3(left, gain_ref[0:SAMPLE_TOTAL, low:], NT)


def update_kernel(transform_ref, cells_ref, out_ref):
    transform = halves(transform_ref[...])
    for r in range(0, 8, 2):
        at = [pl.ds(r + i, SAMPLE_TOTAL, stride=8) for i in range(2)]
        field = jnp.concatenate([cells_ref[a, :] for a in at], axis=1)
        mean = jnp.sum(field, axis=0, keepdims=True) / SAMPLE_TOTAL
        new = field + dot_split(transform, halves(field - mean), NN)
        for i in range(2):
            out_ref[at[i], :] = new[:, 128 * i : 128 * i + 128]


def stack_kernel(*refs):
    for i, ref in enumerate(refs[:-1]):
        refs[-1][i] = ref[...]


def join_kernel(parts_ref, out_ref, arrived):
    copies = []
    for h in range(2):
        for q in range(4):
            place = out_ref.at[:, 8 * h : 8 * h + 8, 128 * q : 128 * q + 128]
            copies.append(pltpu.make_async_copy(parts_ref.at[4 * h + q], place, arrived.at[4 * h + q]))
    for copy in copies:
        copy.start()
    for copy in copies:
        copy.wait()


def call(kernel, out_shape, scratch=(), grid=(), scalars=0, in_specs=None, out_specs=None, flops=0, bytes_accessed=0, limit=MEDIUM):
    specs = {} if in_specs is None else {"in_specs": in_specs, "out_specs": out_specs}
    return pl.pallas_call(
        kernel,
        out_shape=out_shape,
        grid_spec=pltpu.PrefetchScalarGridSpec(
            num_scalar_prefetch=scalars, grid=grid, scratch_shapes=list(scratch), **specs
        ),
        compiler_params=pltpu.CompilerParams(vmem_limit_bytes=limit),
        cost_estimate=pl.CostEstimate(flops=flops, bytes_accessed=bytes_accessed, transcendentals=0),
    )


def spec(shape, *axes):
    places = tuple(axes) + (None,) * (len(shape) - len(axes))
    return pl.BlockSpec(shape, lambda i, *scalars: tuple(0 if p is None else i for p in places))


def body(prior_samples, neighbour_weights, obs_cell, obs_value, obs_var, block_order):
    f32 = jnp.float32
    members, rows, width = prior_samples.shape
    mem_count, cell_count = lax.axis_size("mem"), lax.axis_size("cell")
    me = lax.axis_index("mem")
    base = (lax.axis_index("cell") * rows).reshape(1)
    shape = jax.ShapeDtypeStruct
    steps = 2
    step = members // steps
    side = 4
    forward = [(i, i + 1) for i in range(cell_count - 1)]
    backward = [(i + 1, i) for i in range(cell_count - 1)]
    swap = [(i, i ^ 1) for i in range(mem_count)]

    def along_x(value, d):
        return lax.ppermute(value, "mem", [(i, (i + 2 * d) % mem_count) for i in range(mem_count)])

    def ring(value, phase, d):
        def target(m, i):
            z, y = i % side, i // side
            if (m + phase) % 2 == 0:
                z = (z + d) % side
            else:
                y = (y + d) % side
            return m * cell_count + y * side + z

        places = [(m, i) for m in range(mem_count) for i in range(cell_count)]
        return lax.ppermute(value, ("mem", "cell"), [(m * cell_count + i, target(m, i)) for m, i in places])

    low = lax.ppermute(prior_samples[:, rows - 1, :], "cell", forward)
    high = lax.ppermute(prior_samples[:, 0, :], "cell", backward)
    smem = pl.BlockSpec(memory_space=pltpu.SMEM)
    seen_shape = shape((members, ALL_OBS), f32)
    pieces, seen = call(
        forecast_kernel,
        (shape((mem_count, members, 8, 128), f32), seen_shape),
        [
            pltpu.VMEM((width, ALL_OBS), jnp.bfloat16),
            pltpu.VMEM((step * rows, width), f32),
        ],
        grid=(steps,),
        in_specs=[
            smem,
            smem,
            spec((step, rows, width), 0),
            spec((4, rows, width)),
            spec(obs_cell.shape),
        ],
        out_specs=[spec((mem_count, step, 8, 128), None, 0), spec((step, ALL_OBS), 0)],
        flops=2_000_000_000,
        bytes_accessed=4_000_000,
        limit=LARGE,
    )(block_order, base, prior_samples, neighbour_weights, obs_cell)
    seen = call(
        halo_kernel,
        seen_shape,
        grid=(1,),
        in_specs=[
            smem,
            smem,
            spec((members, ALL_OBS)),
            spec((members, width)),
            spec((members, width)),
            spec((4, rows, width)),
            spec(obs_cell.shape),
        ],
        out_specs=spec((members, ALL_OBS)),
        limit=SMALL,
    )(block_order, base, seen, low, high, neighbour_weights, obs_cell)

    tiles = spec((4 * members * 8, 128), 0)
    pieces = pl.pallas_call(
        edge_kernel,
        out_shape=shape((mem_count * members * 8, 128), f32),
        grid=(2,),
        in_specs=[tiles, spec((4, rows, width)), spec((members, width)), spec((members, width))],
        out_specs=tiles,
        input_output_aliases={0: 0},
        compiler_params=pltpu.CompilerParams(vmem_limit_bytes=MEDIUM),
    )(pieces.reshape(mem_count * members * 8, 128), neighbour_weights, low, high)
    pieces = pieces.reshape(mem_count, members, 8, 128)

    for phase in range(2):
        others = [ring(seen, phase, d) for d in (1, 3, 2)]
        if phase == 0:
            pieces, *others = lax.optimization_barrier([pieces] + others)
        seen = call(sum_kernel, seen_shape, limit=SMALL)(seen, *others)
    one, three, two = along_x(seen, 1), along_x(seen, 3), along_x(seen, 2)
    one, two, three, pieces = lax.optimization_barrier((one, two, three, pieces))
    cells = lax.all_to_all(pieces, "mem", 0, 0)
    seen = call(stack_kernel, shape((4, members, ALL_OBS), f32), limit=SMALL)(seen, one, two, three)
    other = lax.ppermute(seen, "mem", swap)

    square = (ALL_OBS, ALL_OBS)
    transform = call(
        transform_kernel,
        shape(square, f32),
        [
            pltpu.VMEM(square, f32),
            pltpu.VMEM((SAMPLE_TOTAL + 8, ALL_OBS), f32),
            pltpu.VMEM((SAMPLE_TOTAL + 8, ALL_OBS), f32),
            pltpu.VMEM(square, f32),
            pltpu.VMEM(square, f32),
        ],
        grid=(1,),
        scalars=2,
        in_specs=[
            spec((4, members, ALL_OBS)),
            spec((4, members, ALL_OBS)),
            spec(obs_value.shape),
            spec(obs_var.shape),
        ],
        out_specs=spec(square),
        flops=20_000_000_000,
        bytes_accessed=2_000_000,
    )(block_order, me.reshape(1), seen, other, obs_value, obs_var)

    cells = cells.reshape(SAMPLE_TOTAL * 8, 128)
    new = call(update_kernel, shape(cells.shape, f32), flops=3_000_000_000, bytes_accessed=4_000_000)(
        transform, cells
    )
    new = lax.all_to_all(new.reshape(mem_count, members, 8, 128), "mem", 0, 0)
    anywhere = pl.BlockSpec(memory_space=pl.ANY)
    return call(
        join_kernel,
        shape(prior_samples.shape, f32),
        [pltpu.SemaphoreType.DMA((8,))],
        grid=(1,),
        in_specs=[anywhere],
        out_specs=anywhere,
        bytes_accessed=4_000_000,
        limit=SMALL,
    )(new)


def solution(mesh):
    return jax.shard_map(
        body,
        mesh=mesh,
        in_specs=(P("mem", "cell", None), P(None, "cell", None), P(), P(), P(), P()),
        out_specs=P("mem", "cell", None),
        check_vma=False,
    )
```

```python
import functools

import jax
import jax.numpy as jnp
from jax import lax
from jax.experimental import pallas as pl
from jax.experimental.pallas import tpu as pltpu
from jax.sharding import PartitionSpec as P

SAMPLE_TOTAL = 512
NOBS = 128
ALL_OBS = 512
HIGHEST = lax.Precision.HIGHEST
NT = (((1,), (1,)), ((), ()))
TN = (((0,), (0,)), ((), ()))
NN = (((1,), (0,)), ((), ()))
LARGE = 60 * 1024 * 1024
MEDIUM = 20 * 1024 * 1024
SMALL = 8 * 1024 * 1024


def halves(value):
    high = value.astype(jnp.bfloat16)
    low = (value - high.astype(jnp.float32)).astype(jnp.bfloat16)
    return high, low


def dot_split(left, right, dims):
    f32 = jnp.float32
    left_high, left_low = left
    right_high, right_low = right
    small = lax.dot_general(left_low, right_high, dims, preferred_element_type=f32)
    small = small + lax.dot_general(left_high, right_low, dims, preferred_element_type=f32)
    return small + lax.dot_general(left_high, right_high, dims, preferred_element_type=f32)


def dot3(left, right, dims):
    return dot_split(halves(left), halves(right), dims)


def dot6(left, right, dims):
    return lax.dot_general(
        left, right, dims, precision=HIGHEST, preferred_element_type=jnp.float32
    )


def forecast_kernel(order_ref, base_ref, x_ref, weight_ref, cell_ref, piece_ref, own_ref, pick_ref, flat_ref):
    members, rows, width = x_ref.shape
    col_at = lax.broadcasted_iota(jnp.int32, (rows, width), 1)
    row_at = lax.broadcasted_iota(jnp.int32, (rows, width), 0)
    east, west, north, south = [weight_ref[i] for i in range(4)]
    cell = jnp.concatenate([cell_ref[pl.ds(order_ref[j], 1), :] for j in range(order_ref.shape[0])], axis=1)
    at_row = (cell >> 9) - base_ref[0]

    @pl.when(pl.program_id(0) == 0)
    def _():
        at_col = cell & (width - 1)
        pick = lax.broadcasted_iota(jnp.int32, (width, ALL_OBS), 0) == at_col
        pick_ref[...] = pick.astype(jnp.bfloat16)

    def member(m, carry):
        x = x_ref[m]
        to_east = jnp.where(col_at == width - 1, 0.0, pltpu.roll(x, width - 1, 1))
        to_west = jnp.where(col_at == 0, 0.0, pltpu.roll(x, 1, 1))
        to_north = jnp.where(row_at == 0, 0.0, pltpu.roll(x, 1, 0))
        to_south = jnp.where(row_at == rows - 1, 0.0, pltpu.roll(x, rows - 1, 0))
        f = (
            x
            + east * (to_east - x)
            + west * (to_west - x)
            + north * (to_north - x)
            + south * (to_south - x)
        )
        flat_ref[pl.ds(pl.multiple_of(m * rows, rows), rows), :] = f
        for h in range(2):
            for q in range(4):
                piece_ref[4 * h + q, m] = f[8 * h : 8 * h + 8, 128 * q : 128 * q + 128]
        return carry

    lax.fori_loop(0, members, member, 0, unroll=32)
    own_row = (lax.broadcasted_iota(jnp.int32, (rows, ALL_OBS), 0) == at_row).astype(jnp.float32)
    pick = pick_ref[...]
    part = 8
    for g in range(members // part):
        value = flat_ref[g * part * rows : (g + 1) * part * rows, :]
        total = picked(value, pick).reshape(part, rows, ALL_OBS) * own_row[None]
        own_ref[part * g : part * g + part, :] = jnp.sum(total, axis=1)


def picked(value, pick):
    total = None
    for _ in range(3):
        cut = value.astype(jnp.bfloat16)
        value = value - cut.astype(jnp.float32)
        term = lax.dot_general(cut, pick, NN, preferred_element_type=jnp.float32)
        total = term if total is None else total + term
    return total


def halo_kernel(order_ref, base_ref, own_ref, low_ref, high_ref, weight_ref, cell_ref, out_ref):
    members, width = low_ref.shape
    rows = weight_ref.shape[1]
    cell = jnp.concatenate([cell_ref[pl.ds(order_ref[j], 1), :] for j in range(order_ref.shape[0])], axis=1)
    at_row = (cell >> 9) - base_ref[0]
    pick = lax.broadcasted_iota(jnp.int32, (width, ALL_OBS), 0) == (cell & (width - 1))
    edges = [low_ref[...], high_ref[...], weight_ref[2, 0:8, :], weight_ref[3, rows - 8 :, :]]
    edges = picked(jnp.concatenate(edges, axis=0), pick.astype(jnp.bfloat16))
    first = edges[2 * members : 2 * members + 1] * edges[0:members]
    last = edges[2 * members + 15 : 2 * members + 16] * edges[members : 2 * members]
    out_ref[...] = own_ref[...] + jnp.where(at_row == 0, first, 0.0) + jnp.where(at_row == rows - 1, last, 0.0)


def edge_kernel(piece_ref, weight_ref, low_ref, high_ref, out_ref):
    members = low_ref.shape[0]
    rows = weight_ref.shape[1]
    upper = pl.program_id(0) == 0
    out_ref[...] = piece_ref[...]
    weight = jnp.where(upper, weight_ref[2, 0:1, :], weight_ref[3, rows - 1 : rows, :])
    change = weight * jnp.where(upper, low_ref[...], high_ref[...])

    def add(first):
        for q in range(4):
            at = pl.ds(members * 8 * q + first, members, stride=8)
            out_ref[at, :] = out_ref[at, :] + change[:, 128 * q : 128 * q + 128]

    pl.when(upper)(lambda: add(0))
    pl.when(jnp.logical_not(upper))(lambda: add(7))


def sum_kernel(*refs):
    total = refs[0][...]
    for ref in refs[1:-1]:
        total = total + ref[...]
    refs[-1][...] = total


def over_rows(value, row):
    return jnp.broadcast_to(value[row : row + 1, :], (8, NOBS))


def over_lanes(value, lane):
    return jnp.broadcast_to(value[:, lane : lane + 1], (8, NOBS))


def factor(block, root):
    count = NOBS // 8
    sub = lax.broadcasted_iota(jnp.int32, (8, NOBS), 0)
    lane = lax.broadcasted_iota(jnp.int32, (8, NOBS), 1)
    rows = [block[8 * i : 8 * i + 8, :] for i in range(count)]
    shifted = [(lane == sub + 8 * i).astype(jnp.float32) for i in range(count)]
    inverse = [None] * count
    for b in range(count):
        panel = rows[b]
        column = [over_lanes(panel, 8 * b + k) for k in range(8)]
        done = jnp.zeros((8, NOBS), jnp.float32)
        plus = shifted[b]
        inv_roots = []
        for k in range(8):
            at = 8 * b + k
            pivot = over_rows(column[k], k)
            inv_root = lax.rsqrt(pivot)
            inv = pl.reciprocal(pivot)
            inv_roots.append(inv_root)
            row = jnp.where(lane == at, 1.0, over_rows(panel, k))
            done = jnp.where(sub == k, row * inv_root, done)
            away = jnp.where(sub == k, -1.0, column[k])
            panel = jnp.where((sub == k) | (lane == at), 0.0, panel) - (away * row) * inv
            plus_row = over_rows(plus, k) / (pivot * inv_root + over_rows(root[8 * b : 8 * b + 8, :], k))
            below = jnp.where(sub > k, column[k] * inv_root, 0.0)
            plus = jnp.where(sub == k, plus_row, plus - below * plus_row)
            for j in range(k + 1, 8):
                step = away * over_rows(column[j], k)
                column[j] = jnp.where(sub == k, 0.0, column[j]) - step * inv
        inverse[b] = jnp.where(lane <= sub + 8 * b, done, 0.0)
        shifted[b] = plus
        if b == count - 1:
            break
        for k in reversed(range(8)):
            above = jnp.where(sub < k, over_lanes(done, 8 * b + k), 0.0)
            row = over_rows(plus, k) * inv_roots[k]
            plus = jnp.where(sub == k, row, plus - above * row)
        panel_rows = [over_rows(panel, k) for k in range(8)]
        plus_rows = [over_rows(plus, k) for k in range(8)]
        inside = (lane >= 8 * b) & (lane < 8 * b + 8)
        for r in range(b + 1, count):
            left = [over_lanes(rows[r], 8 * b + k) for k in range(8)]
            new = jnp.where(inside, 0.0, rows[r])
            new_shifted = shifted[r]
            for k in range(8):
                new = new - left[k] * panel_rows[k]
                new_shifted = new_shifted - left[k] * plus_rows[k]
            rows[r] = new
            shifted[r] = new_shifted
    return jnp.concatenate(inverse, axis=0), jnp.concatenate(shifted, axis=0)


def transform_kernel(
    block_ref, me_ref, seen_ref, other_ref, value_ref, var_ref,
    out_ref, cov_ref, state_ref, gain_ref, minus_ref, total_ref,
):
    n = ALL_OBS
    blocks = n // NOBS
    turns, share = seen_ref.shape[0], seen_ref.shape[1]
    value = jnp.concatenate([value_ref[pl.ds(block_ref[j], 1), :] for j in range(blocks)], axis=1)
    var = jnp.concatenate([var_ref[pl.ds(block_ref[j], 1), :] for j in range(blocks)], axis=1)
    total = seen_ref[0] + other_ref[0]
    for d in range(1, turns):
        total = total + seen_ref[d] + other_ref[d]
    mean = jnp.sum(total, axis=0, keepdims=True) / SAMPLE_TOTAL

    me = me_ref[0]

    def at(turn, other):
        place = (me + 2 * (turns - turn)) & (2 * turns - 1)
        place = place ^ 1 if other else place
        return pl.ds(pl.multiple_of(place * share, share), share)

    for d in range(turns):
        state_ref[at(d, False), :] = seen_ref[d] - mean
        state_ref[at(d, True), :] = other_ref[d] - mean
    state_ref[SAMPLE_TOTAL:, :] = jnp.broadcast_to(value - mean, (8, n))
    anomaly = state_ref[0:SAMPLE_TOTAL, :]
    minus_ref[...] = anomaly
    eye = lax.broadcasted_iota(jnp.int32, (NOBS, NOBS), 0) == lax.broadcasted_iota(jnp.int32, (NOBS, NOBS), 1)
    for j in range(blocks):
        low, high = NOBS * j, NOBS * (j + 1)
        cov = dot6(anomaly[:, low:], anomaly[:, low:high], TN) / (SAMPLE_TOTAL - 1)
        cov_ref[low:high, low:high] = cov[:NOBS] + jnp.where(eye, var[:, low:high], 0.0)
        if high < n:
            cov_ref[high:, low:high] = cov[NOBS:]
    for j in range(blocks):
        low, high = NOBS * j, NOBS * (j + 1)
        if j == blocks - 1:
            mean_step = gain_ref[SAMPLE_TOTAL : SAMPLE_TOTAL + 1, :low]
            left = (mean_step - minus_ref[:, :low]) * (1.0 / (SAMPLE_TOTAL - 1))
            total_ref[...] = dot3(left, gain_ref[0:SAMPLE_TOTAL, :low], NT)
        root = jnp.sqrt(jnp.broadcast_to(var[:, low:high], (NOBS, NOBS))).T
        inv_low, inv_sum = factor(cov_ref[low:high, low:high], root)
        rest = high < n
        if rest:
            below = dot6(cov_ref[high:, low:high], inv_low, NT)
            for at in range(high, n, NOBS):
                change = dot6(below[at - high :], below[at - high : at - high + NOBS], NT)
                cov_ref[at:, at : at + NOBS] = cov_ref[at:, at : at + NOBS] - change
        gain = dot6(state_ref[:, low:high], inv_low, NT)
        minus = dot6(minus_ref[:, low:high], inv_sum, NT)
        gain_ref[:, low:high] = gain
        if rest:
            state_ref[:, high:] = state_ref[:, high:] - dot6(gain, below, NT)
            minus_ref[:, high:] = minus_ref[:, high:] - dot6(minus, below, NT)
        minus_ref[:, low:high] = minus
    low = n - NOBS
    left = (gain_ref[SAMPLE_TOTAL : SAMPLE_TOTAL + 1, low:] - minus_ref[:, low:]) * (1.0 / (SAMPLE_TOTAL - 1))
    out_ref[...] = total_ref[...] + dot3(left, gain_ref[0:SAMPLE_TOTAL, low:], NT)


def update_kernel(transform_ref, cells_ref, out_ref):
    high, low = halves(transform_ref[...])
    both = jnp.concatenate([high, low], axis=0)
    for r in range(0, 8, 2):
        at = [pl.ds(r + i, SAMPLE_TOTAL, stride=8) for i in range(2)]
        field = jnp.concatenate([cells_ref[a, :] for a in at], axis=1)
        mean = jnp.sum(field, axis=0, keepdims=True) / SAMPLE_TOTAL
        field_high, field_low = halves(field - mean)
        change = lax.dot_general(both, field_high, NN, preferred_element_type=jnp.float32)
        small = lax.dot_general(high, field_low, NN, preferred_element_type=jnp.float32)
        new = field + ((change[SAMPLE_TOTAL:] + small) + change[:SAMPLE_TOTAL])
        for i in range(2):
            out_ref[at[i], :] = new[:, 128 * i : 128 * i + 128]


def stack_kernel(*refs):
    for i, ref in enumerate(refs[:-1]):
        refs[-1][i] = ref[...]


def join_kernel(parts_ref, out_ref, arrived):
    copies = []
    for h in range(2):
        for q in range(4):
            place = out_ref.at[:, 8 * h : 8 * h + 8, 128 * q : 128 * q + 128]
            copies.append(pltpu.make_async_copy(parts_ref.at[4 * h + q], place, arrived.at[4 * h + q]))
    for copy in copies:
        copy.start()
    for copy in copies:
        copy.wait()


def call(kernel, out_shape, scratch=(), grid=(), scalars=0, in_specs=None, out_specs=None, flops=0, bytes_accessed=0, limit=MEDIUM):
    specs = {} if in_specs is None else {"in_specs": in_specs, "out_specs": out_specs}
    return pl.pallas_call(
        kernel,
        out_shape=out_shape,
        grid_spec=pltpu.PrefetchScalarGridSpec(
            num_scalar_prefetch=scalars, grid=grid, scratch_shapes=list(scratch), **specs
        ),
        compiler_params=pltpu.CompilerParams(vmem_limit_bytes=limit),
        cost_estimate=pl.CostEstimate(flops=flops, bytes_accessed=bytes_accessed, transcendentals=0),
    )


def spec(shape, *axes):
    places = tuple(axes) + (None,) * (len(shape) - len(axes))
    return pl.BlockSpec(shape, lambda i, *scalars: tuple(0 if p is None else i for p in places))


def body(prior_samples, neighbour_weights, obs_cell, obs_value, obs_var, block_order):
    f32 = jnp.float32
    members, rows, width = prior_samples.shape
    mem_count, cell_count = lax.axis_size("mem"), lax.axis_size("cell")
    me = lax.axis_index("mem")
    base = (lax.axis_index("cell") * rows).reshape(1)
    shape = jax.ShapeDtypeStruct
    steps = 2
    step = members // steps
    side = 4
    forward = [(i, i + 1) for i in range(cell_count - 1)]
    backward = [(i + 1, i) for i in range(cell_count - 1)]
    swap = [(i, i ^ 1) for i in range(mem_count)]

    def along_x(value, d):
        return lax.ppermute(value, "mem", [(i, (i + 2 * d) % mem_count) for i in range(mem_count)])

    def ring(value, phase, d):
        def target(m, i):
            z, y = i % side, i // side
            if (m + phase) % 2 == 0:
                z = (z + d) % side
            else:
                y = (y + d) % side
            return m * cell_count + y * side + z

        places = [(m, i) for m in range(mem_count) for i in range(cell_count)]
        return lax.ppermute(value, ("mem", "cell"), [(m * cell_count + i, target(m, i)) for m, i in places])

    low = lax.ppermute(prior_samples[:, rows - 1, :], "cell", forward)
    high = lax.ppermute(prior_samples[:, 0, :], "cell", backward)
    smem = pl.BlockSpec(memory_space=pltpu.SMEM)
    seen_shape = shape((members, ALL_OBS), f32)
    pieces, seen = call(
        forecast_kernel,
        (shape((mem_count, members, 8, 128), f32), seen_shape),
        [
            pltpu.VMEM((width, ALL_OBS), jnp.bfloat16),
            pltpu.VMEM((step * rows, width), f32),
        ],
        grid=(steps,),
        in_specs=[
            smem,
            smem,
            spec((step, rows, width), 0),
            spec((4, rows, width)),
            spec(obs_cell.shape),
        ],
        out_specs=[spec((mem_count, step, 8, 128), None, 0), spec((step, ALL_OBS), 0)],
        flops=2_000_000_000,
        bytes_accessed=4_000_000,
        limit=LARGE,
    )(block_order, base, prior_samples, neighbour_weights, obs_cell)
    seen = call(
        halo_kernel,
        seen_shape,
        grid=(1,),
        in_specs=[
            smem,
            smem,
            spec((members, ALL_OBS)),
            spec((members, width)),
            spec((members, width)),
            spec((4, rows, width)),
            spec(obs_cell.shape),
        ],
        out_specs=spec((members, ALL_OBS)),
        limit=SMALL,
    )(block_order, base, seen, low, high, neighbour_weights, obs_cell)

    tiles = spec((4 * members * 8, 128), 0)
    pieces = pl.pallas_call(
        edge_kernel,
        out_shape=shape((mem_count * members * 8, 128), f32),
        grid=(2,),
        in_specs=[tiles, spec((4, rows, width)), spec((members, width)), spec((members, width))],
        out_specs=tiles,
        input_output_aliases={0: 0},
        compiler_params=pltpu.CompilerParams(vmem_limit_bytes=MEDIUM),
    )(pieces.reshape(mem_count * members * 8, 128), neighbour_weights, low, high)
    pieces = pieces.reshape(mem_count, members, 8, 128)

    for phase in range(2):
        others = [ring(seen, phase, d) for d in (1, 3, 2)]
        if phase == 0:
            pieces, *others = lax.optimization_barrier([pieces] + others)
        seen = call(sum_kernel, seen_shape, limit=SMALL)(seen, *others)
    one, three, two = along_x(seen, 1), along_x(seen, 3), along_x(seen, 2)
    one, two, three, pieces = lax.optimization_barrier((one, two, three, pieces))
    cells = lax.all_to_all(pieces, "mem", 0, 0)
    seen = call(stack_kernel, shape((4, members, ALL_OBS), f32), limit=SMALL)(seen, one, two, three)
    other = lax.ppermute(seen, "mem", swap)

    square = (ALL_OBS, ALL_OBS)
    transform = call(
        transform_kernel,
        shape(square, f32),
        [
            pltpu.VMEM(square, f32),
            pltpu.VMEM((SAMPLE_TOTAL + 8, ALL_OBS), f32),
            pltpu.VMEM((SAMPLE_TOTAL + 8, ALL_OBS), f32),
            pltpu.VMEM(square, f32),
            pltpu.VMEM(square, f32),
        ],
        grid=(1,),
        scalars=2,
        in_specs=[
            spec((4, members, ALL_OBS)),
            spec((4, members, ALL_OBS)),
            spec(obs_value.shape),
            spec(obs_var.shape),
        ],
        out_specs=spec(square),
        flops=20_000_000_000,
        bytes_accessed=2_000_000,
    )(block_order, me.reshape(1), seen, other, obs_value, obs_var)

    cells = cells.reshape(SAMPLE_TOTAL * 8, 128)
    new = call(update_kernel, shape(cells.shape, f32), flops=3_000_000_000, bytes_accessed=4_000_000)(
        transform, cells
    )
    new = lax.all_to_all(new.reshape(mem_count, members, 8, 128), "mem", 0, 0)
    anywhere = pl.BlockSpec(memory_space=pl.ANY)
    return call(
        join_kernel,
        shape(prior_samples.shape, f32),
        [pltpu.SemaphoreType.DMA((8,))],
        grid=(1,),
        in_specs=[anywhere],
        out_specs=anywhere,
        bytes_accessed=4_000_000,
        limit=SMALL,
    )(new)


def solution(mesh):
    return jax.shard_map(
        body,
        mesh=mesh,
        in_specs=(P("mem", "cell", None), P(None, "cell", None), P(), P(), P(), P()),
        out_specs=P("mem", "cell", None),
        check_vma=False,
    )
```
